512 devices in a mesh: dp: 16 (over y, core), expert: 32 (over z, x).
Axes of the slice: x: 4, y: 8, z: 8, core: 2. Of those that a mesh axis runs over, the one named last changes fastest.
Arguments:
- inputs: bfloat16 [2, 65536, 2048], P(None, ('dp', 'expert')), may hold values from -24 to 24
- cotangents: bfloat16 [2, 65536, 2048], P(None, ('dp', 'expert')), may hold values from -24 to 24
- gates: bfloat16 [2, 65536], P(None, ('dp', 'expert')), may hold values from 0.099609375 to 1
- routing: int32 [2, 65536, 1], P(None, ('dp', 'expert')), may hold values from 0 to 15; in each aligned block of 128 rows (0 to 127, 128 to 255, ..., all dimensions but the last counted through in order) at most 12 rows name the same one
- w_gate: bfloat16 [2048, 8192], P('dp', 'expert'), may hold values from -0.125 to 0.125
- w_up: bfloat16 [2048, 8192], P('dp', 'expert'), may hold values from -0.125 to 0.125
- w_down: bfloat16 [8192, 2048], P('expert', 'dp'), may hold values from -0.25 to 0.25
Outputs:
- grad_inputs: bfloat16 [2, 65536, 2048], P(None, ('dp', 'expert'))
- grad_gates: bfloat16 [2, 65536], P(None, ('dp', 'expert'))
- grad_w_gate: float32 [2048, 8192], P('dp', 'expert')
- grad_w_up: float32 [2048, 8192], P('dp', 'expert')
- grad_w_down: float32 [8192, 2048], P('expert', 'dp')
The draws below stay inside these ranges and needn't reach their ends.
Inputs may be any that keep to these rules, and one draw needn't show every extreme that they name: `routing`: in one layer, no expert is named by more than 12 of the 128 tokens of one device; some device's tokens name one expert exactly 12 times.
All inputs are finite; a program needn't handle non-finite values.
Results may differ from the reference program's by a relative error of at most 0.022.
Values may be sent and summed in bfloat16 or wider, within the bound.
No kernel may reach another device: no remote copies, remote signals or barrier semaphores. Data moves between devices by JAX's collectives and lax.ppermute only.
A program may use at most 128 MiB of HBM per device.

```python
import math
import jax
import jax.numpy as jnp
import numpy as np
from jax import lax

D = 2048
H = 512
LAYERS = 2
TOK_DEV = 128
HALF = 256
EXPERTS = 16
CAP = 12
TOKENS = 65536
N_DP = 16
N_EXPERT = 32


def raised(drawn, key, source, target, parts, factor):
    def block_of(axis_at):
        return (jnp.arange(drawn.shape[axis_at]) // (drawn.shape[axis_at] // parts)).reshape((-1,) + (1,) * (drawn.ndim - 1 - axis_at))

    near = jax.random.permutation(key, parts)[block_of(target)]
    other_side = (block_of(target) + parts // 2) % parts
    return jnp.where((block_of(source) == near) | (block_of(source) == other_side), factor * drawn, drawn)


def levels(key, shape, cuts, least, high):
    loudness, own = 1.0, jax.random.fold_in(key, 6)
    for dim, parts in cuts:
        heights = jnp.exp(jax.random.uniform(jax.random.fold_in(own, dim), (parts,), jnp.float32, least / len(cuts), high / len(cuts)))
        loudness = loudness * jnp.repeat(heights, shape[dim] // parts).reshape([-1 if axis == dim else 1 for axis in range(len(shape))])
    return loudness


def deal_out(rng, own, number, rows, number_of, top, most, skew):
    order = jax.random.permutation(rng, number_of)
    heavy_load, common = shares(number_of, rows * top, most, skew, True), shares(number_of, rows * top, most, skew, False)
    places = jnp.arange(number_of)

    def named(sizes, turn):
        used = int((sizes > 0).sum())
        fixed = max(1, used // 4)
        shifted = fixed + (places - fixed + turn * (used - fixed)) % max(1, number_of - fixed)
        return jnp.zeros((number_of,), jnp.int32).at[order[jnp.where(places < fixed, places, shifted)]].set(jnp.asarray(sizes, jnp.int32))

    sizes = jnp.where(number % 4 == 0, named(heavy_load, number // 4), named(common, number - number // 4 - 1))
    mixed = jax.random.permutation(jax.random.fold_in(own, 3), number_of)
    giver, receiver = mixed[0:number_of // 2 * 2:2], mixed[1:number_of // 2 * 2:2]
    slack = jnp.minimum(sizes[giver] - 1, most - sizes[receiver]) // 2
    slack = jnp.where((giver == order[0]) | (receiver == order[0]) | (sizes[receiver] == 0), 0, jnp.maximum(slack, 0))
    shifted = jax.random.randint(jax.random.fold_in(own, 4), (number_of // 2,), 0, 1 << 20) % (slack + 1)
    sizes = sizes.at[giver].add(-shifted).at[receiver].add(shifted)
    members = jnp.searchsorted(jnp.cumsum(sizes), jnp.arange(rows * top), side="right").astype(jnp.int32)
    table = members.reshape(top, rows).T
    table = table[jax.random.permutation(jax.random.fold_in(own, 1), rows)]
    turn = jax.random.randint(jax.random.fold_in(own, 2), (rows, 1), 0, top)
    return jnp.take_along_axis(table, (jnp.arange(top)[None, :] + turn) % top, axis=1)


def shares(amount, total, most, slope, full):
    portions = [(1 << 20) // math.isqrt(rank ** slope) + 1 for rank in range(1, amount + 1)]
    largest = most if full else min(most, max(-(-total // amount), total * portions[0] // sum(portions)))
    least = 1 if total - largest >= amount - 1 else 0
    holding, rest = [largest] + [least] * (amount - 1), total - largest - least * (amount - 1)
    while rest > 0:
        movable = [i for i in range(1, amount) if holding[i] < largest] or [i for i in range(1, amount) if holding[i] < most]
        whole, budget = sum([portions[i] for i in movable]), rest
        for i in movable:
            addition = min(most - holding[i], max(1, budget * portions[i] // whole), rest)
            holding[i] = holding[i] + addition
            rest = rest - addition
    return np.array(holding)


def scatter_about(stream_key, dims, scale, bound, pieces=(), kind=jnp.bfloat16):
    loudness = levels(stream_key, dims, pieces, -0.22, 0.18) if pieces else 1.0
    drawn = jax.random.normal(stream_key, dims, jnp.float32) * scale * loudness
    return jnp.minimum(jnp.maximum(drawn, -bound), bound).astype(kind)


def bell_draw_with(own_key, dims, deviation, bound, shards, heavy, held_as=jnp.bfloat16):
    drawn = deviation * jax.random.normal(own_key, dims, jnp.float32)
    if shards:
        drawn = drawn * levels(own_key, dims, shards, -0.22, 0.18)
    return jnp.clip(raised(drawn, jax.random.fold_in(own_key, 3), *heavy), -bound, bound).astype(held_as)


def setup_inputs(seed: int = 0) -> dict:
    splits = jax.random.split(jax.random.key(seed), 8)
    inputs = bell_draw_with(splits[0], (LAYERS, TOKENS, D), 1.0, 24.0, ((1, 512),), (1, 2, 512, 6.0))
    cotangents = bell_draw_with(splits[1], (LAYERS, TOKENS, D), 1.0, 24.0, ((1, 512),), (1, 2, 512, 6.0))
    gates = jnp.clip(jnp.exp(math.log(1.0) - 2.306499 * jax.random.uniform(splits[2], (LAYERS, TOKENS), jnp.float32) ** levels(splits[2], (LAYERS, TOKENS), ((1, 512),), -0.2, 0.2)), 0.099609375, 1.0).astype(jnp.bfloat16)
    routing_keys = jax.random.split(jax.random.fold_in(splits[3], 1), LAYERS * TOKENS // TOK_DEV)
    routing_turns = jax.random.permutation(jax.random.fold_in(splits[3], 3), LAYERS * TOKENS // TOK_DEV)
    routing = jax.vmap(lambda own, number: deal_out(jax.random.fold_in(splits[3], 2), own, number, TOK_DEV, EXPERTS, 1, CAP, 2))(routing_keys, routing_turns).reshape((LAYERS, TOKENS, 1))
    w_gate = scatter_about(splits[4], (D, EXPERTS * H), D ** -0.5, 0.125, ((0, 16), (1, 32)))
    w_up = scatter_about(splits[5], (D, EXPERTS * H), D ** -0.5, 0.125, ((0, 16), (1, 32)))
    w_down = scatter_about(splits[6], (EXPERTS * H, D), H ** -0.5, 0.25, ((0, 32), (1, 16)))
    return {"inputs": inputs, "cotangents": cotangents, "gates": gates, "routing": routing, "w_gate": w_gate, "w_up": w_up, "w_down": w_down}


def rounded(value):
    return lax.optimization_barrier(value.astype(jnp.bfloat16)).astype(jnp.float32)


def group_terms(tokens_in, grads_in, gate_in, route_in, gate_four, up_four, down_four):
    count = tokens_in.shape[0]
    span = N_EXPERT * CAP
    onehot = (route_in[:, None] == jnp.arange(EXPERTS, dtype=jnp.int32)[None, :]).astype(jnp.int32)
    ranks = jnp.cumsum(onehot.reshape(N_EXPERT, TOK_DEV, EXPERTS), axis=1).reshape(count, EXPERTS) - 1
    placed = jnp.sum(onehot * ranks, axis=1).astype(jnp.int32)
    source = (jnp.arange(count, dtype=jnp.int32) // TOK_DEV).astype(jnp.int32)
    where_to = (route_in * span + source * CAP + placed).astype(jnp.int32)
    token_rows = jnp.zeros((EXPERTS * span, D), jnp.float32).at[where_to].set(tokens_in.astype(jnp.float32)).reshape(EXPERTS, span, D)
    grad_rows = jnp.zeros((EXPERTS * span, D), jnp.float32).at[where_to].set(grads_in.astype(jnp.float32)).reshape(EXPERTS, span, D)
    gate_rows = jnp.zeros((EXPERTS * span,), jnp.float32).at[where_to].set(gate_in.astype(jnp.float32)).reshape(EXPERTS, span)
    gate_f = gate_four.astype(jnp.float32)
    up_f = up_four.astype(jnp.float32)
    down_f = down_four.astype(jnp.float32)
    gate_pre = jnp.einsum('erd,dehk->ehrk', token_rows, gate_f)
    up_value = jnp.einsum('erd,dehk->ehrk', token_rows, up_f)
    back_hidden = jnp.einsum('erd,ehkd->ehrk', grad_rows, down_f)
    sigmoid_gate = jax.nn.sigmoid(gate_pre)
    swish_gate = gate_pre * sigmoid_gate
    hidden = swish_gate * up_value
    scale = gate_rows[:, None, :, None]
    gate_parts = rounded(jnp.sum(hidden * back_hidden, axis=-1))
    gate_grad_rows = jnp.sum(gate_parts, axis=1).astype(jnp.bfloat16)
    scaled = rounded(scale * hidden)
    back_scaled = scale * back_hidden
    grad_pre = rounded(back_scaled * up_value * sigmoid_gate * (1.0 + gate_pre * (1.0 - sigmoid_gate)))
    grad_up = rounded(back_scaled * swish_gate)
    term_down = jnp.einsum('ehrk,erd->ehkd', scaled, grad_rows)
    term_gate = jnp.einsum('erd,ehrk->dehk', token_rows, grad_pre)
    term_up = jnp.einsum('erd,ehrk->dehk', token_rows, grad_up)
    input_parts = jnp.einsum('ehrk,dehk->ehrd', grad_pre, gate_f) + jnp.einsum('ehrk,dehk->ehrd', grad_up, up_f)
    input_rows = jnp.sum(rounded(input_parts), axis=1).astype(jnp.bfloat16)
    grad_tokens = input_rows.reshape(EXPERTS * span, D)[where_to]
    grad_gate_tokens = gate_grad_rows.reshape(EXPERTS * span)[where_to]
    return grad_tokens, grad_gate_tokens, term_gate, term_up, term_down


def per_group(array):
    count = N_EXPERT * TOK_DEV
    return jnp.swapaxes(array.reshape((LAYERS, N_DP, count) + array.shape[2:]), 0, 1)


def reference(inputs, cotangents, gates, routing, w_gate, w_up, w_down):
    gate_four = w_gate.reshape(D, EXPERTS, 2, HALF)
    up_four = w_up.reshape(D, EXPERTS, 2, HALF)
    down_four = w_down.reshape(EXPERTS, 2, HALF, D)
    stacked = (per_group(inputs), per_group(cotangents), per_group(gates), per_group(routing[:, :, 0]))

    def visit(carry, group):
        tokens_in, grads_in, gate_in, route_in = group
        sums = [jnp.zeros(c.shape, jnp.float32) for c in carry]
        token_outs = []
        gate_outs = []
        for layer in range(LAYERS):
            result = group_terms(tokens_in[layer], grads_in[layer], gate_in[layer], route_in[layer].astype(jnp.int32), gate_four, up_four, down_four)
            token_outs.append(result[0])
            gate_outs.append(result[1])
            sums = [s + t for s, t in zip(sums, result[2:])]
        new_carry = tuple(c + rounded(s) for c, s in zip(carry, sums))
        return new_carry, (jnp.stack(token_outs), jnp.stack(gate_outs))

    init = (jnp.zeros((D, EXPERTS, 2, HALF), jnp.float32), jnp.zeros((D, EXPERTS, 2, HALF), jnp.float32), jnp.zeros((EXPERTS, 2, HALF, D), jnp.float32))
    carry, outs = lax.scan(visit, init, stacked)
    grad_inputs = jnp.swapaxes(outs[0], 0, 1).reshape(LAYERS, TOKENS, D)
    grad_gates = jnp.swapaxes(outs[1], 0, 1).reshape(LAYERS, TOKENS)
    grad_w_gate = carry[0].reshape(D, EXPERTS * H)
    grad_w_up = carry[1].reshape(D, EXPERTS * H)
    grad_w_down = carry[2].reshape(EXPERTS * H, D)
    return (grad_inputs, grad_gates, grad_w_gate, grad_w_up, grad_w_down)
```

```python
import functools

import jax
import jax.numpy as jnp
from jax import lax
from jax.experimental import pallas as pl
from jax.experimental.pallas import tpu as pltpu
from jax.sharding import Mesh
from jax.sharding import PartitionSpec as P

VMEM_LIMIT = 48 * 1024 * 1024
CONTRACT_ROWS = (((0,), (0,)), ((), ()))
CONTRACT_COLS = (((1,), (1,)), ((), ()))


def whole(memory_space=pltpu.VMEM):
    return pl.BlockSpec(memory_space=memory_space)


def cost(flops, moved):
    return pl.CostEstimate(flops=flops, bytes_accessed=moved, transcendentals=0)


def slot_match(route, experts, capacity):
    layers, tokens = route.shape
    span = layers * capacity
    upto = (
        lax.broadcasted_iota(jnp.int32, (tokens, tokens), 0)
        <= lax.broadcasted_iota(jnp.int32, (tokens, tokens), 1)
    ).astype(jnp.bfloat16)
    numbers = lax.broadcasted_iota(jnp.int32, (experts, tokens), 0)
    keys = []
    for layer in range(layers):
        row = route[layer : layer + 1, :]
        onehot = (numbers == row).astype(jnp.float32)
        ranks = jnp.dot(onehot.astype(jnp.bfloat16), upto, preferred_element_type=jnp.float32)
        rank = jnp.sum(onehot * ranks, axis=0, keepdims=True).astype(jnp.int32) - 1
        key = row * span + layer * capacity + rank
        keys.append(jnp.where(rank < capacity, key, -1))
    key = jnp.concatenate(keys, axis=1)
    slots = lax.broadcasted_iota(jnp.int32, (experts * span, layers * tokens), 0)
    return slots == key


def pack_kernel(x_ref, dy_ref, gate_ref, route_ref, out_ref, table_ref, *, capacity):
    layers, tokens, columns = x_ref.shape
    experts = out_ref.shape[0] // (layers * capacity)
    step = pl.program_id(0)

    @pl.when(step == 0)
    def _():
        table_ref[...] = slot_match(route_ref[...], experts, capacity).astype(jnp.bfloat16)

    @pl.when(step == 2)
    def _():
        scale = jnp.concatenate([gate_ref[layer : layer + 1, :] for layer in range(layers)], axis=1)
        table_ref[...] = table_ref[...] * scale

    def fill(src_ref):
        got = jnp.dot(
            table_ref[...],
            src_ref[...].reshape(layers * tokens, columns),
            preferred_element_type=jnp.float32,
        )
        out_ref[...] = got.astype(jnp.bfloat16)

    pl.when(step < 2)(lambda: fill(x_ref))
    pl.when(step >= 2)(lambda: fill(dy_ref))


def fixed(shape):
    return pl.BlockSpec(shape, lambda t: (0,) * len(shape))


def pack(x, dy, gates, route, experts, capacity):
    layers, tokens, width = x.shape
    rows, half = experts * layers * capacity, width // 2
    block = (layers, tokens, half)
    return pl.pallas_call(
        functools.partial(pack_kernel, capacity=capacity),
        grid=(4,),
        out_shape=jax.ShapeDtypeStruct((rows, 2 * width), jnp.bfloat16),
        in_specs=[
            pl.BlockSpec(block, lambda t: (0, 0, jnp.minimum(t, 1))),
            pl.BlockSpec(block, lambda t: (0, 0, jnp.maximum(t - 2, 0))),
            fixed(gates.shape),
            fixed(route.shape),
        ],
        out_specs=pl.BlockSpec((rows, half), lambda t: (0, t)),
        scratch_shapes=[pltpu.VMEM((rows, layers * tokens), jnp.bfloat16)],
        compiler_params=pltpu.CompilerParams(vmem_limit_bytes=VMEM_LIMIT),
        cost_estimate=cost(2 * rows * layers * tokens * 2 * width, 5 << 20),
        name="pack",
    )(x, dy, gates, route)


def forward_kernel(core_ref, recv_ref, weight_ref, grads_ref, hidden_ref, gate_ref, term_ref):
    width, columns = weight_ref.shape
    unit = columns // 6
    gate_sum = 0.0
    for part in range(2):
        base = part * 3 * unit
        pre = jnp.dot(
            recv_ref[:, :width],
            weight_ref[:, base : base + 2 * unit],
            preferred_element_type=jnp.float32,
        )
        back = jnp.dot(
            recv_ref[:, width:],
            weight_ref[:, base + 2 * unit : base + 3 * unit],
            preferred_element_type=jnp.float32,
        )
        gate_pre, up_value = pre[:, :unit], pre[:, unit:]
        sigmoid = jax.nn.sigmoid(gate_pre)
        swish = gate_pre * sigmoid
        hidden = swish * up_value
        gate_sum = gate_sum + jnp.sum(hidden * back, axis=1, keepdims=True)
        grad_pre = back * up_value * sigmoid * (1.0 + gate_pre * (1.0 - sigmoid))
        grads_ref[:, 2 * part * unit : (2 * part + 1) * unit] = grad_pre.astype(jnp.bfloat16)
        grads_ref[:, (2 * part + 1) * unit : (2 * part + 2) * unit] = (back * swish).astype(
            jnp.bfloat16
        )
        hidden_ref[:, part * unit : (part + 1) * unit] = hidden.astype(jnp.bfloat16)
    gate_ref[...] = jnp.broadcast_to(gate_sum, gate_ref.shape).astype(jnp.bfloat16)
    weight_terms(recv_ref, grads_ref, hidden_ref, 1 - core_ref[0], term_ref, None)


def weight_terms(recv_ref, grads_ref, hidden_ref, side, out_ref, add_ref):
    half, columns = out_ref.shape
    unit = columns // 6
    piece = 128

    @pl.loop(0, half // (2 * piece))
    def _(at):
        rows = pl.ds(pl.multiple_of(at * 2 * piece, 2 * piece), 2 * piece)

        def pick(offset):
            first = pl.multiple_of(offset + (4 * at + side) * piece, piece)
            second = pl.multiple_of(offset + (4 * at + 2 + side) * piece, piece)
            return jnp.concatenate(
                [recv_ref[:, pl.ds(first, piece)], recv_ref[:, pl.ds(second, piece)]], axis=1
            )

        up = lax.dot_general(
            pick(0), grads_ref[...], CONTRACT_ROWS, preferred_element_type=jnp.float32
        )
        down = lax.dot_general(
            pick(2 * half), hidden_ref[...], CONTRACT_ROWS, preferred_element_type=jnp.float32
        )
        for part in range(2):
            base = part * 3 * unit
            first = up[:, 2 * part * unit : (2 * part + 2) * unit]
            second = down[:, part * unit : (part + 1) * unit]
            if add_ref is not None:
                first = first + add_ref[rows, base : base + 2 * unit].astype(jnp.float32)
                second = second + add_ref[rows, base + 2 * unit : base + 3 * unit].astype(jnp.float32)
            out_ref[rows, base : base + 2 * unit] = first.astype(jnp.bfloat16)
            out_ref[rows, base + 2 * unit : base + 3 * unit] = second.astype(jnp.bfloat16)


def forward(core, recv, weights):
    rows = recv.shape[0]
    width, columns = weights.shape
    return pl.pallas_call(
        forward_kernel,
        out_shape=(
            jax.ShapeDtypeStruct((rows, columns // 6 * 4), jnp.bfloat16),
            jax.ShapeDtypeStruct((rows, columns // 3), jnp.bfloat16),
            jax.ShapeDtypeStruct((rows, 128), jnp.bfloat16),
            jax.ShapeDtypeStruct((width // 2, columns), jnp.bfloat16),
        ),
        in_specs=[whole(pltpu.SMEM), whole(), whole()],
        out_specs=(whole(),) * 4,
        compiler_params=pltpu.CompilerParams(vmem_limit_bytes=VMEM_LIMIT),
        cost_estimate=cost(3 * rows * width * columns, 14 << 20),
        name="forward",
    )(core, recv, weights)


def input_kernel(grads_ref, weight_ref, gate_ref, out_ref):
    width, columns = weight_ref.shape
    unit = columns // 6
    chunk = min(256, width)

    @pl.loop(0, width // chunk)
    def _(at):
        start = pl.ds(pl.multiple_of(at * chunk, chunk), chunk)
        got = 0.0
        for part in range(2):
            got = got + lax.dot_general(
                grads_ref[:, 2 * part * unit : (2 * part + 2) * unit],
                weight_ref[start, 3 * part * unit : (3 * part + 2) * unit],
                CONTRACT_COLS,
                preferred_element_type=jnp.float32,
            )
        out_ref[:, start] = got.astype(jnp.bfloat16)

    out_ref[:, width:] = gate_ref[...]


def input_terms(grads, weights, gate):
    rows = grads.shape[0]
    width, columns = weights.shape
    return pl.pallas_call(
        input_kernel,
        out_shape=jax.ShapeDtypeStruct((rows, width + gate.shape[1]), jnp.bfloat16),
        in_specs=[whole()] * 3,
        out_specs=whole(),
        compiler_params=pltpu.CompilerParams(vmem_limit_bytes=VMEM_LIMIT),
        cost_estimate=cost(4 * rows * width * columns // 3, 9 << 20),
        name="input_terms",
    )(grads, weights, gate)


def own_kernel(core_ref, recv_ref, grads_ref, hidden_ref, arrived_ref, out_ref):
    weight_terms(recv_ref, grads_ref, hidden_ref, core_ref[0], out_ref, arrived_ref)


def own_terms(core, recv, grads, hidden, arrived):
    rows = recv.shape[0]
    half, columns = arrived.shape
    return pl.pallas_call(
        own_kernel,
        out_shape=jax.ShapeDtypeStruct((half, columns), jnp.bfloat16),
        in_specs=[whole(pltpu.SMEM)] + [whole()] * 4,
        out_specs=whole(),
        compiler_params=pltpu.CompilerParams(vmem_limit_bytes=VMEM_LIMIT),
        cost_estimate=cost(2 * rows * half * columns, 10 << 20),
        name="own_terms",
    )(core, recv, grads, hidden, arrived)


def unpack_kernel(back_ref, sum_ref, gate_ref, route_ref, out_ref, gate_out_ref, table_ref, *, capacity):
    layers, tokens = route_ref.shape
    experts = back_ref.shape[0] // (layers * capacity)

    @pl.when(pl.program_id(0) == 0)
    def _():
        match = slot_match(route_ref[...], experts, capacity)
        table_ref[...] = match.astype(jnp.bfloat16)
        sums = sum_ref[:, 0:1].astype(jnp.float32)
        picked = jnp.sum(jnp.where(match, sums, 0.0), axis=0, keepdims=True)
        for layer in range(layers):
            gate = gate_ref[layer : layer + 1, :].astype(jnp.float32)
            value = picked[:, layer * tokens : (layer + 1) * tokens] / gate
            gate_out_ref[layer : layer + 1, :] = value.astype(jnp.bfloat16)

    got = lax.dot_general(
        table_ref[...], back_ref[...], CONTRACT_ROWS, preferred_element_type=jnp.float32
    ).astype(jnp.bfloat16)
    out_ref[...] = got.reshape(out_ref.shape)


def unpack(back, gates, route, capacity):
    rows, columns = back.shape
    layers, tokens = route.shape
    width = columns - 128
    steps = 4
    block = width // steps
    return pl.pallas_call(
        functools.partial(unpack_kernel, capacity=capacity),
        grid=(steps,),
        out_shape=(
            jax.ShapeDtypeStruct((layers, tokens, width), jnp.bfloat16),
            jax.ShapeDtypeStruct((layers, tokens), jnp.bfloat16),
        ),
        in_specs=[
            pl.BlockSpec((rows, block), lambda t: (0, t)),
            pl.BlockSpec((rows, 128), lambda t: (0, width // 128)),
            fixed(gates.shape),
            fixed(route.shape),
        ],
        out_specs=(
            pl.BlockSpec((layers, tokens, block), lambda t: (0, 0, t)),
            fixed((layers, tokens)),
        ),
        scratch_shapes=[pltpu.VMEM((rows, layers * tokens), jnp.bfloat16)],
        compiler_params=pltpu.CompilerParams(vmem_limit_bytes=VMEM_LIMIT),
        cost_estimate=cost(2 * rows * layers * tokens * width, 3 << 20),
        name="unpack",
    )(back, back, gates, route)


def local(inputs, cotangents, gates, routing, w_gate, w_up, w_down):
    experts = lax.axis_size("e")
    layers, tokens, width = inputs.shape
    capacity = 3 * tokens // (2 * experts)
    unit = w_gate.shape[1]
    route = routing[:, :, 0]
    core = lax.axis_index("c").astype(jnp.int32).reshape(1)
    swap = [(0, 1), (1, 0)]

    mine = jnp.concatenate([w_gate, w_up, w_down.T], axis=1)
    both = jnp.concatenate([mine, lax.ppermute(mine, "k", swap)], axis=1)
    weights = lax.all_gather(both, ("y", "c"), axis=0, tiled=True)

    sent = pack(inputs, cotangents, gates, route, experts, capacity)
    recv = lax.all_to_all(
        sent.reshape(experts, layers * capacity, 2 * width), "e", 0, 0, tiled=True
    ).reshape(experts * layers * capacity, 2 * width)

    grads, hidden, gate_sum, term = forward(core, recv, weights)
    arrived = lax.ppermute(term, "c", swap)
    back = input_terms(grads, weights, gate_sum)
    total = own_terms(core, recv, grads, hidden, arrived)
    total, back = lax.optimization_barrier((total, back))
    reduced = lax.psum_scatter(total, "y", scatter_dimension=0, tiled=True)
    back = lax.all_to_all(
        back.reshape(experts, layers * capacity, back.shape[1]), "e", 0, 0, tiled=True
    ).reshape(back.shape)
    grad_inputs, grad_gates = unpack(back, gates, route, capacity)
    reduced, grad_gates = lax.optimization_barrier((reduced, grad_gates))

    partner = lax.ppermute(reduced[:, 3 * unit :], "k", swap)
    final = reduced[:, : 3 * unit].astype(jnp.float32) + partner.astype(jnp.float32)
    return (
        grad_inputs,
        grad_gates,
        final[:, :unit],
        final[:, unit : 2 * unit],
        final[:, 2 * unit :].T,
    )


def solution(mesh):
    count, peers = mesh.devices.shape
    fine = Mesh(mesh.devices.reshape(count // 2, 2, peers // 2, 2), ("y", "c", "e", "k"))
    dp, expert, both = ("y", "c"), ("e", "k"), ("y", "c", "e", "k")
    return jax.shard_map(
        local,
        mesh=fine,
        in_specs=(
            P(None, both, None),
            P(None, both, None),
            P(None, both),
            P(None, both, None),
            P(dp, expert),
            P(dp, expert),
            P(expert, dp),
        ),
        out_specs=(
            P(None, both, None),
            P(None, both),
            P(dp, expert),
            P(dp, expert),
            P(expert, dp),
        ),
        check_vma=False,
    )
```

```python
import functools

import jax
import jax.numpy as jnp
from jax import lax
from jax.experimental import pallas as pl
from jax.experimental.pallas import tpu as pltpu
from jax.sharding import Mesh
from jax.sharding import PartitionSpec as P

MIB = 1024 * 1024
PACK_LIMIT = 56 * MIB
CONTRACT_ROWS = (((0,), (0,)), ((), ()))
CONTRACT_COLS = (((1,), (1,)), ((), ()))


def whole(memory_space=pltpu.VMEM):
    return pl.BlockSpec(memory_space=memory_space)


def cost(flops, moved):
    return pl.CostEstimate(flops=flops, bytes_accessed=moved, transcendentals=0)


def slot_match(route, experts, capacity):
    layers, tokens = route.shape
    span = layers * capacity
    upto = (
        lax.broadcasted_iota(jnp.int32, (tokens, tokens), 0)
        <= lax.broadcasted_iota(jnp.int32, (tokens, tokens), 1)
    ).astype(jnp.bfloat16)
    numbers = lax.broadcasted_iota(jnp.int32, (experts, tokens), 0)
    keys = []
    for layer in range(layers):
        row = route[layer : layer + 1, :]
        onehot = (numbers == row).astype(jnp.float32)
        ranks = jnp.dot(onehot.astype(jnp.bfloat16), upto, preferred_element_type=jnp.float32)
        rank = jnp.sum(onehot * ranks, axis=0, keepdims=True).astype(jnp.int32) - 1
        key = row * span + layer * capacity + rank
        keys.append(jnp.where(rank < capacity, key, -1))
    key = jnp.concatenate(keys, axis=1)
    slots = lax.broadcasted_iota(jnp.int32, (experts * span, layers * tokens), 0)
    return slots == key


def pack_kernel(
    x_hbm, dy_hbm, gate_hbm, route_hbm, out_ref, x_ref, dy_ref, gate_ref, route_ref, sems, *, capacity
):
    layers, tokens, width = x_ref.shape
    rows = out_ref.shape[0]
    experts = rows // (layers * capacity)
    halves = (slice(0, width // 2), slice(width // 2, width))
    moves = [(route_hbm, route_ref), (gate_hbm, gate_ref)]
    for src, dst in ((x_hbm, x_ref), (dy_hbm, dy_ref)):
        moves += [(src.at[:, :, half], dst.at[:, :, half]) for half in halves]
    copies = [pltpu.make_async_copy(src, dst, sems.at[i]) for i, (src, dst) in enumerate(moves)]
    for copy in copies:
        copy.start()
    copies[0].wait()
    match = slot_match(route_ref[...], experts, capacity).astype(jnp.bfloat16)
    copies[1].wait()
    scale = jnp.concatenate([gate_ref[layer : layer + 1, :] for layer in range(layers)], axis=1)
    for i, (src, table) in enumerate(((x_ref, match), (dy_ref, match * scale))):
        for j, half in enumerate(halves):
            copies[2 + 2 * i + j].wait()
            got = jnp.dot(
                table,
                src[:, :, half].reshape(layers * tokens, width // 2),
                preferred_element_type=jnp.float32,
            )
            at = i * width + j * (width // 2)
            out_ref[:, at : at + width // 2] = got.astype(jnp.bfloat16)


def fixed(shape):
    return pl.BlockSpec(shape, lambda t: (0,) * len(shape))


def pack(x, dy, gates, route, experts, capacity):
    layers, tokens, width = x.shape
    rows = experts * layers * capacity
    return pl.pallas_call(
        functools.partial(pack_kernel, capacity=capacity),
        out_shape=jax.ShapeDtypeStruct((rows, 2 * width), jnp.bfloat16),
        in_specs=[whole(pltpu.HBM)] * 4,
        out_specs=whole(),
        scratch_shapes=[
            pltpu.VMEM(x.shape, x.dtype),
            pltpu.VMEM(dy.shape, dy.dtype),
            pltpu.VMEM(gates.shape, gates.dtype),
            pltpu.VMEM(route.shape, route.dtype),
            pltpu.SemaphoreType.DMA((6,)),
        ],
        compiler_params=pltpu.CompilerParams(vmem_limit_bytes=PACK_LIMIT),
        cost_estimate=cost(2 * rows * layers * tokens * 2 * width, 5 * MIB),
        name="pack",
    )(x, dy, gates, route)


def join_kernel(wg_ref, wu_ref, wd_ref, out_ref):
    unit = wg_ref.shape[1]
    out_ref[:, :unit] = wg_ref[...]
    out_ref[:, unit : 2 * unit] = wu_ref[...]
    out_ref[:, 2 * unit :] = wd_ref[...].T


def join(w_gate, w_up, w_down):
    piece, unit = w_gate.shape
    return pl.pallas_call(
        join_kernel,
        out_shape=jax.ShapeDtypeStruct((piece, 3 * unit), jnp.bfloat16),
        in_specs=[whole()] * 3,
        out_specs=whole(),
        compiler_params=pltpu.CompilerParams(vmem_limit_bytes=PACK_LIMIT),
        cost_estimate=cost(0, MIB),
        name="join",
    )(w_gate, w_up, w_down)


def forward_kernel(core_ref, recv_ref, weight_ref, grads_ref, hidden_ref, gate_ref, term_ref):
    width, columns = weight_ref.shape
    unit = columns // 6
    gate_sum = 0.0
    for part in range(2):
        base = part * 3 * unit
        pre = jnp.dot(
            recv_ref[:, :width],
            weight_ref[:, base : base + 2 * unit],
            preferred_element_type=jnp.float32,
        )
        back = jnp.dot(
            recv_ref[:, width:],
            weight_ref[:, base + 2 * unit : base + 3 * unit],
            preferred_element_type=jnp.float32,
        )
        gate_pre, up_value = pre[:, :unit], pre[:, unit:]
        sigmoid = jax.nn.sigmoid(gate_pre)
        swish = gate_pre * sigmoid
        hidden = swish * up_value
        gate_sum = gate_sum + jnp.sum(hidden * back, axis=1, keepdims=True)
        grad_pre = back * up_value * sigmoid * (1.0 + gate_pre * (1.0 - sigmoid))
        grads_ref[:, 2 * part * unit : (2 * part + 1) * unit] = grad_pre.astype(jnp.bfloat16)
        grads_ref[:, (2 * part + 1) * unit : (2 * part + 2) * unit] = (back * swish).astype(
            jnp.bfloat16
        )
        hidden_ref[:, part * unit : (part + 1) * unit] = hidden.astype(jnp.bfloat16)
    gate_ref[...] = jnp.broadcast_to(gate_sum, gate_ref.shape).astype(jnp.bfloat16)
    weight_terms(recv_ref, grads_ref, hidden_ref, 1 - core_ref[0], term_ref, None)


def weight_terms(recv_ref, grads_ref, hidden_ref, side, out_ref, add_ref):
    half, columns = out_ref.shape
    unit = columns // 6
    piece = 128
    blocks = min(4, half // piece)

    for at in range(0, half // piece, blocks):
        rows = slice(at * piece, (at + blocks) * piece)

        def pick(offset):
            starts = [
                pl.multiple_of(offset + (2 * (at + j) + side) * piece, piece) for j in range(blocks)
            ]
            return jnp.concatenate([recv_ref[:, pl.ds(start, piece)] for start in starts], axis=1)

        up = lax.dot_general(
            pick(0), grads_ref[...], CONTRACT_ROWS, preferred_element_type=jnp.float32
        )
        down = lax.dot_general(
            pick(2 * half), hidden_ref[...], CONTRACT_ROWS, preferred_element_type=jnp.float32
        )
        for part in range(2):
            base = part * 3 * unit
            first = up[:, 2 * part * unit : (2 * part + 2) * unit]
            second = down[:, part * unit : (part + 1) * unit]
            if add_ref is not None:
                first = first + add_ref[rows, base : base + 2 * unit].astype(jnp.float32)
                second = second + add_ref[rows, base + 2 * unit : base + 3 * unit].astype(jnp.float32)
            out_ref[rows, base : base + 2 * unit] = first.astype(jnp.bfloat16)
            out_ref[rows, base + 2 * unit : base + 3 * unit] = second.astype(jnp.bfloat16)


def forward(core, recv, weights):
    rows = recv.shape[0]
    width, columns = weights.shape
    return pl.pallas_call(
        forward_kernel,
        out_shape=(
            jax.ShapeDtypeStruct((rows, columns // 6 * 4), jnp.bfloat16),
            jax.ShapeDtypeStruct((rows, columns // 3), jnp.bfloat16),
            jax.ShapeDtypeStruct((rows, 128), jnp.bfloat16),
            jax.ShapeDtypeStruct((width // 2, columns), jnp.bfloat16),
        ),
        in_specs=[whole(pltpu.SMEM), whole(), whole()],
        out_specs=(whole(),) * 4,
        compiler_params=pltpu.CompilerParams(vmem_limit_bytes=24 * MIB),
        cost_estimate=cost(3 * rows * width * columns, 14 << 20),
        name="forward",
    )(core, recv, weights)


def input_kernel(grads_ref, weight_ref, gate_ref, out_ref):
    width, columns = weight_ref.shape
    unit = columns // 6
    chunk = width // 2
    for at in range(2):
        rows = slice(at * chunk, (at + 1) * chunk)
        got = 0.0
        for part in range(2):
            got = got + lax.dot_general(
                grads_ref[:, 2 * part * unit : (2 * part + 2) * unit],
                weight_ref[rows, 3 * part * unit : (3 * part + 2) * unit],
                CONTRACT_COLS,
                preferred_element_type=jnp.float32,
            )
        out_ref[:, rows] = got.astype(jnp.bfloat16)
    out_ref[:, width:] = gate_ref[...]


def input_terms(grads, weights, gate):
    rows = grads.shape[0]
    width, columns = weights.shape
    return pl.pallas_call(
        input_kernel,
        out_shape=jax.ShapeDtypeStruct((rows, width + gate.shape[1]), jnp.bfloat16),
        in_specs=[whole()] * 3,
        out_specs=whole(),
        compiler_params=pltpu.CompilerParams(vmem_limit_bytes=16 * MIB),
        cost_estimate=cost(4 * rows * width * columns // 3, 9 << 20),
        name="input_terms",
    )(grads, weights, gate)


def own_kernel(core_ref, recv_ref, grads_ref, hidden_ref, arrived_ref, out_ref):
    weight_terms(recv_ref, grads_ref, hidden_ref, core_ref[0], out_ref, arrived_ref)


def own_terms(core, recv, grads, hidden, arrived):
    rows = recv.shape[0]
    half, columns = arrived.shape
    return pl.pallas_call(
        own_kernel,
        out_shape=jax.ShapeDtypeStruct((half, columns), jnp.bfloat16),
        in_specs=[whole(pltpu.SMEM)] + [whole()] * 4,
        out_specs=whole(),
        compiler_params=pltpu.CompilerParams(vmem_limit_bytes=20 * MIB),
        cost_estimate=cost(2 * rows * half * columns, 10 << 20),
        name="own_terms",
    )(core, recv, grads, hidden, arrived)


def unpack_kernel(back_ref, sum_ref, gate_ref, route_ref, out_ref, gate_out_ref, table_ref, *, capacity):
    layers, tokens = route_ref.shape
    experts = back_ref.shape[0] // (layers * capacity)

    @pl.when(pl.program_id(0) == 0)
    def _():
        match = slot_match(route_ref[...], experts, capacity)
        table_ref[...] = match.astype(jnp.bfloat16)
        sums = sum_ref[:, 0:1].astype(jnp.float32)
        picked = jnp.sum(jnp.where(match, sums, 0.0), axis=0, keepdims=True)
        for layer in range(layers):
            gate = gate_ref[layer : layer + 1, :].astype(jnp.float32)
            value = picked[:, layer * tokens : (layer + 1) * tokens] / gate
            gate_out_ref[layer : layer + 1, :] = value.astype(jnp.bfloat16)

    got = lax.dot_general(
        table_ref[...], back_ref[...], CONTRACT_ROWS, preferred_element_type=jnp.float32
    ).astype(jnp.bfloat16)
    out_ref[...] = got.reshape(out_ref.shape)


def unpack(back, gates, route, capacity):
    rows, columns = back.shape
    layers, tokens = route.shape
    width = columns - 128
    steps = 4
    block = width // steps
    return pl.pallas_call(
        functools.partial(unpack_kernel, capacity=capacity),
        grid=(steps,),
        out_shape=(
            jax.ShapeDtypeStruct((layers, tokens, width), jnp.bfloat16),
            jax.ShapeDtypeStruct((layers, tokens), jnp.bfloat16),
        ),
        in_specs=[
            pl.BlockSpec((rows, block), lambda t: (0, t)),
            pl.BlockSpec((rows, 128), lambda t: (0, width // 128)),
            fixed(gates.shape),
            fixed(route.shape),
        ],
        out_specs=(
            pl.BlockSpec((layers, tokens, block), lambda t: (0, 0, t)),
            fixed((layers, tokens)),
        ),
        scratch_shapes=[pltpu.VMEM((rows, layers * tokens), jnp.bfloat16)],
        compiler_params=pltpu.CompilerParams(vmem_limit_bytes=12 * MIB),
        cost_estimate=cost(2 * rows * layers * tokens * width, 3 << 20),
        name="unpack",
    )(back, back, gates, route)


def finish_kernel(reduced_ref, partner_ref, gate_ref, up_ref, down_ref):
    unit = gate_ref.shape[1]
    for i, ref in enumerate((gate_ref, up_ref, down_ref)):
        at = slice(i * unit, (i + 1) * unit)
        value = reduced_ref[:, at].astype(jnp.float32) + partner_ref[:, at].astype(jnp.float32)
        ref[...] = value if i < 2 else value.T


def finish(reduced, partner):
    piece, columns = partner.shape
    unit = columns // 3
    return pl.pallas_call(
        finish_kernel,
        out_shape=(
            jax.ShapeDtypeStruct((piece, unit), jnp.float32),
            jax.ShapeDtypeStruct((piece, unit), jnp.float32),
            jax.ShapeDtypeStruct((unit, piece), jnp.float32),
        ),
        in_specs=[pl.BlockSpec((piece, columns), lambda t: (0, 0))] * 2,
        out_specs=(fixed((piece, unit)), fixed((piece, unit)), fixed((unit, piece))),
        grid=(1,),
        compiler_params=pltpu.CompilerParams(vmem_limit_bytes=8 * MIB),
        cost_estimate=cost(piece * columns, MIB),
        name="finish",
    )(reduced, partner)


def local(inputs, cotangents, gates, routing, w_gate, w_up, w_down):
    experts = lax.axis_size("e")
    layers, tokens, width = inputs.shape
    capacity = 3 * tokens // (2 * experts)
    unit = w_gate.shape[1]
    route = routing[:, :, 0]
    core = lax.axis_index("c").astype(jnp.int32).reshape(1)
    swap = [(0, 1), (1, 0)]

    mine = join(w_gate, w_up, w_down)
    paired = lax.ppermute(mine, "k", swap)
    sent = pack(inputs, cotangents, gates, route, experts, capacity)
    paired, sent = lax.optimization_barrier((paired, sent))
    recv = lax.all_to_all(
        sent.reshape(experts, layers * capacity, 2 * width), "e", 0, 0, tiled=True
    ).reshape(experts * layers * capacity, 2 * width)
    both = jnp.concatenate([mine, paired], axis=1)
    weights = lax.all_gather(both, ("y", "c"), axis=0, tiled=True)

    grads, hidden, gate_sum, term = forward(core, recv, weights)
    arrived = lax.ppermute(term, "c", swap)
    back = input_terms(grads, weights, gate_sum)
    hidden, back = lax.optimization_barrier((hidden, back))
    total = own_terms(core, recv, grads, hidden, arrived)
    reduced = lax.psum_scatter(total, "y", scatter_dimension=0, tiled=True)
    back = lax.all_to_all(
        back.reshape(experts, layers * capacity, back.shape[1]), "e", 0, 0, tiled=True
    ).reshape(back.shape)
    grad_inputs, grad_gates = unpack(back, gates, route, capacity)
    reduced, grad_gates = lax.optimization_barrier((reduced, grad_gates))
    partner = lax.ppermute(reduced[:, 3 * unit :], "k", swap)
    return (grad_inputs, grad_gates, *finish(reduced, partner))


def solution(mesh):
    count, peers = mesh.devices.shape
    fine = Mesh(mesh.devices.reshape(count // 2, 2, peers // 2, 2), ("y", "c", "e", "k"))
    dp, expert, both = ("y", "c"), ("e", "k"), ("y", "c", "e", "k")
    return jax.shard_map(
        local,
        mesh=fine,
        in_specs=(
            P(None, both, None),
            P(None, both, None),
            P(None, both),
            P(None, both, None),
            P(dp, expert),
            P(dp, expert),
            P(expert, dp),
        ),
        out_specs=(
            P(None, both, None),
            P(None, both),
            P(dp, expert),
            P(dp, expert),
            P(expert, dp),
        ),
        check_vma=False,
    )
```

```python
import functools

import jax
import jax.numpy as jnp
from jax import lax
from jax.experimental import pallas as pl
from jax.experimental.pallas import tpu as pltpu
from jax.sharding import Mesh
from jax.sharding import PartitionSpec as P

MIB = 1024 * 1024
PACK_LIMIT = 56 * MIB
CONTRACT_ROWS = (((0,), (0,)), ((), ()))
CONTRACT_COLS = (((1,), (1,)), ((), ()))


def whole(memory_space=pltpu.VMEM):
    return pl.BlockSpec(memory_space=memory_space)


def cost(flops, moved):
    return pl.CostEstimate(flops=flops, bytes_accessed=moved, transcendentals=0)


def slot_match(route, experts, capacity):
    layers, tokens = route.shape
    span = layers * capacity
    upto = (
        lax.broadcasted_iota(jnp.int32, (tokens, tokens), 0)
        <= lax.broadcasted_iota(jnp.int32, (tokens, tokens), 1)
    ).astype(jnp.bfloat16)
    numbers = lax.broadcasted_iota(jnp.int32, (experts, tokens), 0)
    keys = []
    for layer in range(layers):
        row = route[layer : layer + 1, :]
        onehot = (numbers == row).astype(jnp.float32)
        ranks = jnp.dot(onehot.astype(jnp.bfloat16), upto, preferred_element_type=jnp.float32)
        rank = jnp.sum(onehot * ranks, axis=0, keepdims=True).astype(jnp.int32) - 1
        key = row * span + layer * capacity + rank
        keys.append(jnp.where(rank < capacity, key, -1))
    key = jnp.concatenate(keys, axis=1)
    slots = lax.broadcasted_iota(jnp.int32, (experts * span, layers * tokens), 0)
    return slots == key


def pack_kernel(
    x_hbm, dy_hbm, gate_hbm, route_hbm, out_hbm,
    x_ref, dy_ref, gate_ref, route_ref, out_ref, sems, out_sems, *, capacity
):
    layers, tokens, width = x_ref.shape
    rows = out_ref.shape[0]
    experts = rows // (layers * capacity)
    halves = (slice(0, width // 2), slice(width // 2, width))
    moves = [(route_hbm, route_ref), (gate_hbm, gate_ref)]
    for src, dst in ((x_hbm, x_ref), (dy_hbm, dy_ref)):
        moves += [(src.at[:, :, half], dst.at[:, :, half]) for half in halves]
    copies = [pltpu.make_async_copy(src, dst, sems.at[i]) for i, (src, dst) in enumerate(moves)]
    for copy in copies:
        copy.start()
    copies[0].wait()
    match = slot_match(route_ref[...], experts, capacity).astype(jnp.bfloat16)
    copies[1].wait()
    scale = jnp.concatenate([gate_ref[layer : layer + 1, :] for layer in range(layers)], axis=1)
    leaving = []
    for i, (src, table) in enumerate(((x_ref, match), (dy_ref, match * scale))):
        for j, half in enumerate(halves):
            copies[2 + 2 * i + j].wait()
            got = jnp.dot(
                table,
                src[:, :, half].reshape(layers * tokens, width // 2),
                preferred_element_type=jnp.float32,
            )
            at = slice(i * width + j * (width // 2), i * width + (j + 1) * (width // 2))
            out_ref[:, at] = got.astype(jnp.bfloat16)
            leaving.append(
                pltpu.make_async_copy(out_ref.at[:, at], out_hbm.at[:, at], out_sems.at[2 * i + j])
            )
            leaving[-1].start()
    for copy in leaving:
        copy.wait()


def fixed(shape):
    return pl.BlockSpec(shape, lambda t: (0,) * len(shape))


def pack(x, dy, gates, route, experts, capacity):
    layers, tokens, width = x.shape
    rows = experts * layers * capacity
    return pl.pallas_call(
        functools.partial(pack_kernel, capacity=capacity),
        out_shape=pltpu.HBM((rows, 2 * width), jnp.bfloat16),
        in_specs=[whole(pl.ANY)] * 4,
        out_specs=whole(pl.ANY),
        scratch_shapes=[
            pltpu.VMEM(x.shape, x.dtype),
            pltpu.VMEM(dy.shape, dy.dtype),
            pltpu.VMEM(gates.shape, gates.dtype),
            pltpu.VMEM(route.shape, route.dtype),
            pltpu.VMEM((rows, 2 * width), jnp.bfloat16),
            pltpu.SemaphoreType.DMA((6,)),
            pltpu.SemaphoreType.DMA((4,)),
        ],
        compiler_params=pltpu.CompilerParams(vmem_limit_bytes=PACK_LIMIT),
        cost_estimate=cost(2 * rows * layers * tokens * 2 * width, 5 * MIB),
        name="pack",
    )(x, dy, gates, route)


def join_kernel(wg_ref, wu_ref, wd_ref, out_ref):
    unit = wg_ref.shape[1]
    out_ref[:, :unit] = wg_ref[...]
    out_ref[:, unit : 2 * unit] = wu_ref[...]
    out_ref[:, 2 * unit :] = wd_ref[...].T


def join(w_gate, w_up, w_down):
    piece, unit = w_gate.shape
    return pl.pallas_call(
        join_kernel,
        out_shape=jax.ShapeDtypeStruct((piece, 3 * unit), jnp.bfloat16),
        in_specs=[whole()] * 3,
        out_specs=whole(),
        compiler_params=pltpu.CompilerParams(vmem_limit_bytes=PACK_LIMIT),
        cost_estimate=cost(0, MIB),
        name="join",
    )(w_gate, w_up, w_down)


def weight_copies(weight_hbm, weight_ref, sems, pieces):
    copies = [
        pltpu.make_async_copy(weight_hbm.at[:, piece], weight_ref.at[:, piece], sems.at[i])
        for i, piece in enumerate(pieces)
    ]
    for copy in copies:
        copy.start()
    return copies


def forward_kernel(
    core_ref, recv_ref, weight_hbm, grads_ref, hidden_ref, gate_ref, term_ref, weight_ref, sems
):
    width, columns = weight_ref.shape
    unit = columns // 6
    pieces = []
    for part in range(2):
        base = part * 3 * unit
        pieces += [slice(base, base + 2 * unit), slice(base + 2 * unit, base + 3 * unit)]
    copies = weight_copies(weight_hbm, weight_ref, sems, pieces)
    gate_sum = 0.0
    for part in range(2):
        copies[2 * part].wait()
        pre = jnp.dot(
            recv_ref[:, :width], weight_ref[:, pieces[2 * part]], preferred_element_type=jnp.float32
        )
        copies[2 * part + 1].wait()
        back = jnp.dot(
            recv_ref[:, width:],
            weight_ref[:, pieces[2 * part + 1]],
            preferred_element_type=jnp.float32,
        )
        gate_pre, up_value = pre[:, :unit], pre[:, unit:]
        sigmoid = jax.nn.sigmoid(gate_pre)
        swish = gate_pre * sigmoid
        hidden = swish * up_value
        gate_sum = gate_sum + jnp.sum(hidden * back, axis=1, keepdims=True)
        grad_pre = back * up_value * sigmoid * (1.0 + gate_pre * (1.0 - sigmoid))
        grads_ref[:, 2 * part * unit : (2 * part + 1) * unit] = grad_pre.astype(jnp.bfloat16)
        grads_ref[:, (2 * part + 1) * unit : (2 * part + 2) * unit] = (back * swish).astype(
            jnp.bfloat16
        )
        hidden_ref[:, part * unit : (part + 1) * unit] = hidden.astype(jnp.bfloat16)
    gate_ref[...] = jnp.broadcast_to(gate_sum, gate_ref.shape).astype(jnp.bfloat16)
    weight_terms(recv_ref, grads_ref, hidden_ref, 1 - core_ref[0], term_ref, None)


def weight_terms(recv_ref, grads_ref, hidden_ref, side, out_ref, add_ref, done=None):
    half, columns = out_ref.shape
    unit = columns // 6
    piece = 128
    blocks = min(4, half // piece)

    for at in range(0, half // piece, blocks):
        rows = slice(at * piece, (at + blocks) * piece)

        def pick(offset):
            starts = [
                pl.multiple_of(offset + (2 * (at + j) + side) * piece, piece) for j in range(blocks)
            ]
            return jnp.concatenate([recv_ref[:, pl.ds(start, piece)] for start in starts], axis=1)

        up = lax.dot_general(
            pick(0), grads_ref[...], CONTRACT_ROWS, preferred_element_type=jnp.float32
        )
        down = lax.dot_general(
            pick(2 * half), hidden_ref[...], CONTRACT_ROWS, preferred_element_type=jnp.float32
        )
        for part in range(2):
            base = part * 3 * unit
            first = up[:, 2 * part * unit : (2 * part + 2) * unit]
            second = down[:, part * unit : (part + 1) * unit]
            if add_ref is not None:
                first = first + add_ref[rows, base : base + 2 * unit].astype(jnp.float32)
                second = second + add_ref[rows, base + 2 * unit : base + 3 * unit].astype(jnp.float32)
            out_ref[rows, base : base + 2 * unit] = first.astype(jnp.bfloat16)
            out_ref[rows, base + 2 * unit : base + 3 * unit] = second.astype(jnp.bfloat16)
        if done is not None:
            done(at // blocks, rows)


def forward(core, recv, weights):
    rows = recv.shape[0]
    width, columns = weights.shape
    return pl.pallas_call(
        forward_kernel,
        out_shape=(
            jax.ShapeDtypeStruct((rows, columns // 6 * 4), jnp.bfloat16),
            jax.ShapeDtypeStruct((rows, columns // 3), jnp.bfloat16),
            jax.ShapeDtypeStruct((rows, 128), jnp.bfloat16),
            jax.ShapeDtypeStruct((width // 2, columns), jnp.bfloat16),
        ),
        in_specs=[whole(pltpu.SMEM), whole(), whole(pl.ANY)],
        out_specs=(whole(),) * 4,
        scratch_shapes=[pltpu.VMEM(weights.shape, weights.dtype), pltpu.SemaphoreType.DMA((4,))],
        compiler_params=pltpu.CompilerParams(vmem_limit_bytes=44 * MIB),
        cost_estimate=cost(3 * rows * width * columns, 14 << 20),
        name="forward",
    )(core, recv, weights)


def input_kernel(grads_ref, weight_hbm, gate_ref, out_ref, weight_ref, sems):
    width, columns = weight_ref.shape
    unit = columns // 6
    chunk = width // 2
    pieces = [slice(3 * part * unit, (3 * part + 2) * unit) for part in range(2)]
    copies = [
        pltpu.make_async_copy(
            weight_hbm.at[pl.ds(at * chunk, chunk), piece],
            weight_ref.at[pl.ds(at * chunk, chunk), piece],
            sems.at[2 * at + part],
        )
        for at in range(2)
        for part, piece in enumerate(pieces)
    ]
    for copy in copies:
        copy.start()
    for at in range(2):
        rows = slice(at * chunk, (at + 1) * chunk)
        got = 0.0
        for part in range(2):
            copies[2 * at + part].wait()
            got = got + lax.dot_general(
                grads_ref[:, 2 * part * unit : (2 * part + 2) * unit],
                weight_ref[rows, pieces[part]],
                CONTRACT_COLS,
                preferred_element_type=jnp.float32,
            )
        out_ref[:, rows] = got.astype(jnp.bfloat16)
    out_ref[:, width:] = gate_ref[...]


def input_terms(grads, weights, gate):
    rows = grads.shape[0]
    width, columns = weights.shape
    return pl.pallas_call(
        input_kernel,
        out_shape=jax.ShapeDtypeStruct((rows, width + gate.shape[1]), jnp.bfloat16),
        in_specs=[whole(), whole(pl.ANY), whole()],
        out_specs=whole(),
        scratch_shapes=[pltpu.VMEM(weights.shape, weights.dtype), pltpu.SemaphoreType.DMA((4,))],
        compiler_params=pltpu.CompilerParams(vmem_limit_bytes=20 * MIB),
        cost_estimate=cost(4 * rows * width * columns // 3, 9 << 20),
        name="input_terms",
    )(grads, weights, gate)


def own_kernel(core_ref, recv_ref, grads_ref, hidden_ref, arrived_ref, out_hbm, out_ref, sems):
    copies = []

    def done(i, rows):
        copies.append(pltpu.make_async_copy(out_ref.at[rows], out_hbm.at[rows], sems.at[i]))
        copies[-1].start()

    weight_terms(recv_ref, grads_ref, hidden_ref, core_ref[0], out_ref, arrived_ref, done)
    for copy in copies:
        copy.wait()


def own_terms(core, recv, grads, hidden, arrived):
    rows = recv.shape[0]
    half, columns = arrived.shape
    return pl.pallas_call(
        own_kernel,
        out_shape=pltpu.HBM((half, columns), jnp.bfloat16),
        in_specs=[whole(pltpu.SMEM)] + [whole()] * 4,
        out_specs=whole(pl.ANY),
        scratch_shapes=[pltpu.VMEM(arrived.shape, jnp.bfloat16), pltpu.SemaphoreType.DMA((2,))],
        compiler_params=pltpu.CompilerParams(vmem_limit_bytes=24 * MIB),
        cost_estimate=cost(2 * rows * half * columns, 10 << 20),
        name="own_terms",
    )(core, recv, grads, hidden, arrived)


def unpack_kernel(back_ref, sum_ref, gate_ref, route_ref, out_ref, gate_out_ref, table_ref, *, capacity):
    layers, tokens = route_ref.shape
    experts = back_ref.shape[0] // (layers * capacity)

    @pl.when(pl.program_id(0) == 0)
    def _():
        match = slot_match(route_ref[...], experts, capacity)
        table_ref[...] = match.astype(jnp.bfloat16)
        sums = sum_ref[:, 0:1].astype(jnp.float32)
        picked = jnp.sum(jnp.where(match, sums, 0.0), axis=0, keepdims=True)
        for layer in range(layers):
            gate = gate_ref[layer : layer + 1, :].astype(jnp.float32)
            value = picked[:, layer * tokens : (layer + 1) * tokens] / gate
            gate_out_ref[layer : layer + 1, :] = value.astype(jnp.bfloat16)

    got = lax.dot_general(
        table_ref[...], back_ref[...], CONTRACT_ROWS, preferred_element_type=jnp.float32
    ).astype(jnp.bfloat16)
    out_ref[...] = got.reshape(out_ref.shape)


def unpack(back, gates, route, capacity):
    rows, columns = back.shape
    layers, tokens = route.shape
    width = columns - 128
    steps = 4
    block = width // steps
    return pl.pallas_call(
        functools.partial(unpack_kernel, capacity=capacity),
        grid=(steps,),
        out_shape=(
            jax.ShapeDtypeStruct((layers, tokens, width), jnp.bfloat16),
            jax.ShapeDtypeStruct((layers, tokens), jnp.bfloat16),
        ),
        in_specs=[
            pl.BlockSpec((rows, block), lambda t: (0, t)),
            pl.BlockSpec((rows, 128), lambda t: (0, width // 128)),
            fixed(gates.shape),
            fixed(route.shape),
        ],
        out_specs=(
            pl.BlockSpec((layers, tokens, block), lambda t: (0, 0, t)),
            fixed((layers, tokens)),
        ),
        scratch_shapes=[pltpu.VMEM((rows, layers * tokens), jnp.bfloat16)],
        compiler_params=pltpu.CompilerParams(vmem_limit_bytes=12 * MIB),
        cost_estimate=cost(2 * rows * layers * tokens * width, 3 << 20),
        name="unpack",
    )(back, back, gates, route)


def finish_kernel(reduced_ref, partner_ref, gate_ref, up_ref, down_ref):
    unit = gate_ref.shape[1]
    for i, ref in enumerate((gate_ref, up_ref, down_ref)):
        at = slice(i * unit, (i + 1) * unit)
        value = reduced_ref[:, at].astype(jnp.float32) + partner_ref[:, at].astype(jnp.float32)
        ref[...] = value if i < 2 else value.T


def finish(reduced, partner):
    piece, columns = partner.shape
    unit = columns // 3
    return pl.pallas_call(
        finish_kernel,
        out_shape=(
            jax.ShapeDtypeStruct((piece, unit), jnp.float32),
            jax.ShapeDtypeStruct((piece, unit), jnp.float32),
            jax.ShapeDtypeStruct((unit, piece), jnp.float32),
        ),
        in_specs=[pl.BlockSpec((piece, columns), lambda t: (0, 0))] * 2,
        out_specs=(fixed((piece, unit)), fixed((piece, unit)), fixed((unit, piece))),
        grid=(1,),
        compiler_params=pltpu.CompilerParams(vmem_limit_bytes=50 * MIB),
        cost_estimate=cost(piece * columns, MIB),
        name="finish",
    )(reduced, partner)


def local(inputs, cotangents, gates, routing, w_gate, w_up, w_down):
    experts = lax.axis_size("e")
    layers, tokens, width = inputs.shape
    capacity = 3 * tokens // (2 * experts)
    unit = w_gate.shape[1]
    route = routing[:, :, 0]
    core = lax.axis_index("c").astype(jnp.int32).reshape(1)
    swap = [(0, 1), (1, 0)]

    mine = join(w_gate, w_up, w_down)
    paired = lax.ppermute(mine, "k", swap)
    sent = pack(inputs, cotangents, gates, route, experts, capacity)
    paired, sent = lax.optimization_barrier((paired, sent))
    recv = lax.all_to_all(
        sent.reshape(experts, layers * capacity, 2 * width), "e", 0, 0, tiled=True
    ).reshape(experts * layers * capacity, 2 * width)
    both = jnp.concatenate([mine, paired], axis=1)
    weights = lax.all_gather(both, ("y", "c"), axis=0, tiled=True)

    grads, hidden, gate_sum, term = forward(core, recv, weights)
    arrived = lax.ppermute(term, "c", swap)
    back = input_terms(grads, weights, gate_sum)
    hidden, back = lax.optimization_barrier((hidden, back))
    total = own_terms(core, recv, grads, hidden, arrived)
    reduced = lax.psum_scatter(total, "y", scatter_dimension=0, tiled=True)
    back = lax.all_to_all(
        back.reshape(experts, layers * capacity, back.shape[1]), "e", 0, 0, tiled=True
    ).reshape(back.shape)
    grad_inputs, grad_gates = unpack(back, gates, route, capacity)
    partner = lax.ppermute(reduced[:, 3 * unit :], "k", swap)
    return (grad_inputs, grad_gates, *finish(reduced, partner))


def solution(mesh):
    count, peers = mesh.devices.shape
    fine = Mesh(mesh.devices.reshape(count // 2, 2, peers // 2, 2), ("y", "c", "e", "k"))
    dp, expert, both = ("y", "c"), ("e", "k"), ("y", "c", "e", "k")
    return jax.shard_map(
        local,
        mesh=fine,
        in_specs=(
            P(None, both, None),
            P(None, both, None),
            P(None, both),
            P(None, both, None),
            P(dp, expert),
            P(dp, expert),
            P(expert, dp),
        ),
        out_specs=(
            P(None, both, None),
            P(None, both),
            P(dp, expert),
            P(dp, expert),
            P(expert, dp),
        ),
        check_vma=False,
    )
```

```python
import functools

import jax
import jax.numpy as jnp
from jax import lax
from jax.experimental import pallas as pl
from jax.experimental.pallas import tpu as pltpu
from jax.sharding import Mesh
from jax.sharding import PartitionSpec as P

MIB = 1024 * 1024
PACK_LIMIT = 56 * MIB
FORWARD_LIMIT = 38 * MIB
CONTRACT_ROWS = (((0,), (0,)), ((), ()))
CONTRACT_COLS = (((1,), (1,)), ((), ()))


def whole(memory_space=pltpu.VMEM):
    return pl.BlockSpec(memory_space=memory_space)


def cost(flops, moved):
    return pl.CostEstimate(flops=flops, bytes_accessed=moved, transcendentals=0)


def slot_match(route, experts, capacity):
    layers, tokens = route.shape
    span = layers * capacity
    upto = (
        lax.broadcasted_iota(jnp.int32, (tokens, tokens), 0)
        <= lax.broadcasted_iota(jnp.int32, (tokens, tokens), 1)
    ).astype(jnp.bfloat16)
    numbers = lax.broadcasted_iota(jnp.int32, (experts, tokens), 0)
    keys = []
    for layer in range(layers):
        row = route[layer : layer + 1, :]
        onehot = (numbers == row).astype(jnp.float32)
        ranks = jnp.dot(onehot.astype(jnp.bfloat16), upto, preferred_element_type=jnp.float32)
        rank = jnp.sum(onehot * ranks, axis=0, keepdims=True).astype(jnp.int32) - 1
        key = row * span + layer * capacity + rank
        keys.append(jnp.where(rank < capacity, key, -1))
    key = jnp.concatenate(keys, axis=1)
    slots = lax.broadcasted_iota(jnp.int32, (experts * span, layers * tokens), 0)
    return slots == key


def pack_kernel(
    x_hbm, dy_hbm, gate_hbm, route_hbm, out_hbm,
    x_ref, dy_ref, gate_ref, route_ref, out_ref, sems, out_sems, *, capacity
):
    layers, tokens, width = x_ref.shape
    rows = out_ref.shape[0]
    experts = rows // (layers * capacity)
    halves = (slice(0, width // 2), slice(width // 2, width))
    moves = [(route_hbm, route_ref), (gate_hbm, gate_ref)]
    for src, dst in ((x_hbm, x_ref), (dy_hbm, dy_ref)):
        moves += [(src.at[:, :, half], dst.at[:, :, half]) for half in halves]
    copies = [pltpu.make_async_copy(src, dst, sems.at[i]) for i, (src, dst) in enumerate(moves)]
    for copy in copies:
        copy.start()
    copies[0].wait()
    match = slot_match(route_ref[...], experts, capacity).astype(jnp.bfloat16)
    copies[1].wait()
    scale = jnp.concatenate([gate_ref[layer : layer + 1, :] for layer in range(layers)], axis=1)
    leaving = []
    for i, (src, table) in enumerate(((x_ref, match), (dy_ref, match * scale))):
        for j, half in enumerate(halves):
            copies[2 + 2 * i + j].wait()
            got = jnp.dot(
                table,
                src[:, :, half].reshape(layers * tokens, width // 2),
                preferred_element_type=jnp.float32,
            )
            at = slice(i * width + j * (width // 2), i * width + (j + 1) * (width // 2))
            out_ref[:, at] = got.astype(jnp.bfloat16)
            leaving.append(
                pltpu.make_async_copy(out_ref.at[:, at], out_hbm.at[:, at], out_sems.at[2 * i + j])
            )
            leaving[-1].start()
    for copy in leaving:
        copy.wait()


def fixed(shape):
    return pl.BlockSpec(shape, lambda t: (0,) * len(shape))


def pack(x, dy, gates, route, experts, capacity):
    layers, tokens, width = x.shape
    rows = experts * layers * capacity
    return pl.pallas_call(
        functools.partial(pack_kernel, capacity=capacity),
        out_shape=pltpu.HBM((rows, 2 * width), jnp.bfloat16),
        in_specs=[whole(pl.ANY)] * 4,
        out_specs=whole(pl.ANY),
        scratch_shapes=[
            pltpu.VMEM(x.shape, x.dtype),
            pltpu.VMEM(dy.shape, dy.dtype),
            pltpu.VMEM(gates.shape, gates.dtype),
            pltpu.VMEM(route.shape, route.dtype),
            pltpu.VMEM((rows, 2 * width), jnp.bfloat16),
            pltpu.SemaphoreType.DMA((6,)),
            pltpu.SemaphoreType.DMA((4,)),
        ],
        compiler_params=pltpu.CompilerParams(vmem_limit_bytes=PACK_LIMIT),
        cost_estimate=cost(2 * rows * layers * tokens * 2 * width, 5 * MIB),
        name="pack",
    )(x, dy, gates, route)


def join_kernel(*refs):
    out_ref = refs[-1]
    unit = refs[0].shape[1]
    for part in range(2):
        gate_ref, up_ref, down_ref = refs[3 * part : 3 * part + 3]
        base = 3 * part * unit
        out_ref[:, base : base + unit] = gate_ref[...]
        out_ref[:, base + unit : base + 2 * unit] = up_ref[...]
        out_ref[:, base + 2 * unit : base + 3 * unit] = down_ref[...].T


def join(own, partner):
    piece, unit = own[0].shape
    return pl.pallas_call(
        join_kernel,
        out_shape=pltpu.HBM((piece, 6 * unit), jnp.bfloat16),
        in_specs=[whole()] * 6,
        out_specs=whole(),
        compiler_params=pltpu.CompilerParams(vmem_limit_bytes=8 * MIB),
        cost_estimate=cost(0, MIB),
        name="join",
    )(*own, *partner)


def weight_copies(weight_hbm, weight_ref, sems, pieces):
    copies = [
        pltpu.make_async_copy(weight_hbm.at[:, piece], weight_ref.at[:, piece], sems.at[i])
        for i, piece in enumerate(pieces)
    ]
    for copy in copies:
        copy.start()
    return copies


def forward_kernel(
    core_ref, recv_ref, weight_hbm, grads_ref, hidden_ref, gate_ref, term_ref, weight_ref, sems
):
    width, columns = weight_ref.shape
    unit = columns // 6
    pieces = []
    for part in range(2):
        base = part * 3 * unit
        pieces += [slice(base, base + 2 * unit), slice(base + 2 * unit, base + 3 * unit)]
    copies = weight_copies(weight_hbm, weight_ref, sems, pieces)
    gate_sum = 0.0
    for part in range(2):
        copies[2 * part].wait()
        pre = jnp.dot(
            recv_ref[:, :width], weight_ref[:, pieces[2 * part]], preferred_element_type=jnp.float32
        )
        copies[2 * part + 1].wait()
        back = jnp.dot(
            recv_ref[:, width:],
            weight_ref[:, pieces[2 * part + 1]],
            preferred_element_type=jnp.float32,
        )
        gate_pre, up_value = pre[:, :unit], pre[:, unit:]
        sigmoid = jax.nn.sigmoid(gate_pre)
        swish = gate_pre * sigmoid
        hidden = swish * up_value
        gate_sum = gate_sum + jnp.sum(hidden * back, axis=1, keepdims=True)
        grad_pre = back * up_value * sigmoid * (1.0 + gate_pre * (1.0 - sigmoid))
        grads_ref[:, 2 * part * unit : (2 * part + 1) * unit] = grad_pre.astype(jnp.bfloat16)
        grads_ref[:, (2 * part + 1) * unit : (2 * part + 2) * unit] = (back * swish).astype(
            jnp.bfloat16
        )
        hidden_ref[:, part * unit : (part + 1) * unit] = hidden.astype(jnp.bfloat16)
    gate_ref[...] = jnp.broadcast_to(gate_sum, gate_ref.shape).astype(jnp.bfloat16)
    weight_terms(recv_ref, grads_ref, hidden_ref, 1 - core_ref[0], term_ref)


def weight_terms(recv_ref, grads_ref, hidden_ref, side, out_ref):
    half, columns = out_ref.shape
    unit = columns // 6
    piece = 128
    blocks = min(4, half // piece)

    for at in range(0, half // piece, blocks):
        rows = slice(at * piece, (at + blocks) * piece)

        def pick(offset):
            starts = [
                pl.multiple_of(offset + (2 * (at + j) + side) * piece, piece) for j in range(blocks)
            ]
            return jnp.concatenate([recv_ref[:, pl.ds(start, piece)] for start in starts], axis=1)

        up = lax.dot_general(
            pick(0), grads_ref[...], CONTRACT_ROWS, preferred_element_type=jnp.float32
        )
        down = lax.dot_general(
            pick(2 * half), hidden_ref[...], CONTRACT_ROWS, preferred_element_type=jnp.float32
        )
        for part in range(2):
            base = part * 3 * unit
            out_ref[rows, base : base + 2 * unit] = up[
                :, 2 * part * unit : (2 * part + 2) * unit
            ].astype(out_ref.dtype)
            out_ref[rows, base + 2 * unit : base + 3 * unit] = down[
                :, part * unit : (part + 1) * unit
            ].astype(out_ref.dtype)


def forward(core, recv, weights):
    rows = recv.shape[0]
    width, columns = weights.shape
    return pl.pallas_call(
        forward_kernel,
        out_shape=(
            jax.ShapeDtypeStruct((rows, columns // 6 * 4), jnp.bfloat16),
            jax.ShapeDtypeStruct((rows, columns // 3), jnp.bfloat16),
            jax.ShapeDtypeStruct((rows, 128), jnp.bfloat16),
            jax.ShapeDtypeStruct((width // 2, columns), jnp.bfloat16),
            pltpu.VMEM(weights.shape, weights.dtype),
        ),
        in_specs=[whole(pltpu.SMEM), whole(), whole(pl.ANY)],
        out_specs=(whole(),) * 5,
        scratch_shapes=[pltpu.SemaphoreType.DMA((4,))],
        compiler_params=pltpu.CompilerParams(vmem_limit_bytes=FORWARD_LIMIT),
        cost_estimate=cost(3 * rows * width * columns, 14 << 20),
        name="forward",
    )(core, recv, weights)


def input_kernel(grads_ref, weight_ref, gate_ref, out_ref):
    width, columns = weight_ref.shape
    unit = columns // 6
    chunk = width // 2
    for at in range(2):
        rows = slice(at * chunk, (at + 1) * chunk)
        got = 0.0
        for part in range(2):
            got = got + lax.dot_general(
                grads_ref[:, 2 * part * unit : (2 * part + 2) * unit],
                weight_ref[rows, 3 * part * unit : (3 * part + 2) * unit],
                CONTRACT_COLS,
                preferred_element_type=jnp.float32,
            )
        out_ref[:, rows] = got.astype(jnp.bfloat16)
    out_ref[:, width:] = gate_ref[...]


def input_terms(grads, weights, gate):
    rows = grads.shape[0]
    width, columns = weights.shape
    return pl.pallas_call(
        input_kernel,
        out_shape=jax.ShapeDtypeStruct((rows, width + gate.shape[1]), jnp.bfloat16),
        in_specs=[whole()] * 3,
        out_specs=whole(),
        compiler_params=pltpu.CompilerParams(vmem_limit_bytes=20 * MIB),
        cost_estimate=cost(4 * rows * width * columns // 3, 9 << 20),
        name="input_terms",
    )(grads, weights, gate)


def own_kernel(core_ref, recv_ref, grads_ref, hidden_ref, out_ref):
    weight_terms(recv_ref, grads_ref, hidden_ref, core_ref[0], out_ref)


def own_terms(core, recv, grads, hidden, columns):
    rows, width = recv.shape
    return pl.pallas_call(
        own_kernel,
        out_shape=jax.ShapeDtypeStruct((width // 4, columns), jnp.float32),
        in_specs=[whole(pltpu.SMEM)] + [whole()] * 3,
        out_specs=whole(),
        compiler_params=pltpu.CompilerParams(vmem_limit_bytes=20 * MIB),
        cost_estimate=cost(rows * width * columns // 2, 10 * MIB),
        name="own_terms",
    )(core, recv, grads, hidden)


def add_kernel(own_ref, arrived_ref, out_hbm, out_ref, sems):
    count = sems.shape[0]
    rows = out_ref.shape[0] // count
    copies = []
    for i in range(count):
        at = slice(i * rows, (i + 1) * rows)
        total = own_ref[at, :] + arrived_ref[at, :].astype(jnp.float32)
        out_ref[at, :] = total.astype(jnp.bfloat16)
        copies.append(pltpu.make_async_copy(out_ref.at[at], out_hbm.at[at], sems.at[i]))
        copies[-1].start()
    for copy in copies:
        copy.wait()


def add(own, arrived):
    return pl.pallas_call(
        add_kernel,
        out_shape=pltpu.HBM(arrived.shape, jnp.bfloat16),
        in_specs=[whole()] * 2,
        out_specs=whole(pl.ANY),
        scratch_shapes=[pltpu.VMEM(arrived.shape, jnp.bfloat16), pltpu.SemaphoreType.DMA((4,))],
        compiler_params=pltpu.CompilerParams(vmem_limit_bytes=20 * MIB),
        cost_estimate=cost(arrived.size, 12 * MIB),
        name="add",
    )(own, arrived)


def unpack_kernel(back_ref, sum_ref, gate_ref, route_ref, out_ref, gate_out_ref, table_ref, *, capacity):
    layers, tokens = route_ref.shape
    experts = back_ref.shape[0] // (layers * capacity)

    @pl.when(pl.program_id(0) == 0)
    def _():
        match = slot_match(route_ref[...], experts, capacity)
        table_ref[...] = match.astype(jnp.bfloat16)
        sums = sum_ref[:, 0:1].astype(jnp.float32)
        picked = jnp.sum(jnp.where(match, sums, 0.0), axis=0, keepdims=True)
        for layer in range(layers):
            gate = gate_ref[layer : layer + 1, :].astype(jnp.float32)
            value = picked[:, layer * tokens : (layer + 1) * tokens] / gate
            gate_out_ref[layer : layer + 1, :] = value.astype(jnp.bfloat16)

    got = lax.dot_general(
        table_ref[...], back_ref[...], CONTRACT_ROWS, preferred_element_type=jnp.float32
    ).astype(jnp.bfloat16)
    out_ref[...] = got.reshape(out_ref.shape)


def unpack(back, gates, route, capacity):
    rows, columns = back.shape
    layers, tokens = route.shape
    width = columns - 128
    steps = 4
    block = width // steps
    return pl.pallas_call(
        functools.partial(unpack_kernel, capacity=capacity),
        grid=(steps,),
        out_shape=(
            jax.ShapeDtypeStruct((layers, tokens, width), jnp.bfloat16),
            jax.ShapeDtypeStruct((layers, tokens), jnp.bfloat16),
        ),
        in_specs=[
            pl.BlockSpec((rows, block), lambda t: (0, t)),
            pl.BlockSpec((rows, 128), lambda t: (0, width // 128)),
            fixed(gates.shape),
            fixed(route.shape),
        ],
        out_specs=(
            pl.BlockSpec((layers, tokens, block), lambda t: (0, 0, t)),
            fixed((layers, tokens)),
        ),
        scratch_shapes=[pltpu.VMEM((rows, layers * tokens), jnp.bfloat16)],
        compiler_params=pltpu.CompilerParams(vmem_limit_bytes=12 * MIB),
        cost_estimate=cost(2 * rows * layers * tokens * width, 3 << 20),
        name="unpack",
    )(back, back, gates, route)


def finish_kernel(reduced_ref, partner_ref, gate_ref, up_ref, down_ref):
    unit = gate_ref.shape[1]
    for i, ref in enumerate((gate_ref, up_ref, down_ref)):
        at = slice(i * unit, (i + 1) * unit)
        value = reduced_ref[:, at].astype(jnp.float32) + partner_ref[:, at].astype(jnp.float32)
        ref[...] = value if i < 2 else value.T


def finish(reduced, partner):
    piece, columns = partner.shape
    unit = columns // 3
    return pl.pallas_call(
        finish_kernel,
        out_shape=(
            jax.ShapeDtypeStruct((piece, unit), jnp.float32),
            jax.ShapeDtypeStruct((piece, unit), jnp.float32),
            jax.ShapeDtypeStruct((unit, piece), jnp.float32),
        ),
        in_specs=[pl.BlockSpec((piece, columns), lambda t: (0, 0))] * 2,
        out_specs=(fixed((piece, unit)), fixed((piece, unit)), fixed((unit, piece))),
        grid=(1,),
        compiler_params=pltpu.CompilerParams(vmem_limit_bytes=50 * MIB),
        cost_estimate=cost(piece * columns, MIB),
        name="finish",
    )(reduced, partner)


def local(inputs, cotangents, gates, routing, w_gate, w_up, w_down):
    experts = lax.axis_size("e")
    layers, tokens, width = inputs.shape
    capacity = 3 * tokens // (2 * experts)
    unit = w_gate.shape[1]
    route = routing[:, :, 0]
    core = lax.axis_index("c").astype(jnp.int32).reshape(1)
    swap = [(0, 1), (1, 0)]

    own = (w_gate, w_up, w_down)
    partner = tuple(lax.ppermute(block, "k", swap) for block in own)
    sent = pack(inputs, cotangents, gates, route, experts, capacity)
    partner, sent = lax.optimization_barrier((partner, sent))
    recv = lax.all_to_all(
        sent.reshape(experts, layers * capacity, 2 * width), "e", 0, 0, tiled=True
    ).reshape(experts * layers * capacity, 2 * width)
    weights = lax.all_gather(join(own, partner), ("y", "c"), axis=0, tiled=True)

    grads, hidden, gate_sum, term, held = forward(core, recv, weights)
    arrived = lax.ppermute(term, "c", swap)
    back = input_terms(grads, held, gate_sum)
    hidden, back = lax.optimization_barrier((hidden, back))
    total = own_terms(core, recv, grads, hidden, weights.shape[1])
    total = add(total, arrived)
    reduced = lax.psum_scatter(total, "y", scatter_dimension=0, tiled=True)
    back = lax.all_to_all(
        back.reshape(experts, layers * capacity, back.shape[1]), "e", 0, 0, tiled=True
    ).reshape(back.shape)
    grad_inputs, grad_gates = unpack(back, gates, route, capacity)
    partner = lax.ppermute(reduced[:, 3 * unit :], "k", swap)
    return (grad_inputs, grad_gates, *finish(reduced, partner))


def solution(mesh):
    count, peers = mesh.devices.shape
    fine = Mesh(mesh.devices.reshape(count // 2, 2, peers // 2, 2), ("y", "c", "e", "k"))
    dp, expert, both = ("y", "c"), ("e", "k"), ("y", "c", "e", "k")
    return jax.shard_map(
        local,
        mesh=fine,
        in_specs=(
            P(None, both, None),
            P(None, both, None),
            P(None, both),
            P(None, both, None),
            P(dp, expert),
            P(dp, expert),
            P(expert, dp),
        ),
        out_specs=(
            P(None, both, None),
            P(None, both),
            P(dp, expert),
            P(dp, expert),
            P(expert, dp),
        ),
        check_vma=False,
    )
```

```python
import functools

import jax
import jax.numpy as jnp
from jax import lax
from jax.experimental import pallas as pl
from jax.experimental.pallas import tpu as pltpu
from jax.sharding import Mesh
from jax.sharding import PartitionSpec as P

MIB = 1024 * 1024
PACK_LIMIT = 56 * MIB
FORWARD_LIMIT = 38 * MIB
JOIN_LIMIT = 60 * MIB
CONTRACT_ROWS = (((0,), (0,)), ((), ()))
CONTRACT_COLS = (((1,), (1,)), ((), ()))


def whole(memory_space=pltpu.VMEM):
    return pl.BlockSpec(memory_space=memory_space)


def cost(flops, moved):
    return pl.CostEstimate(flops=flops, bytes_accessed=moved, transcendentals=0)


def slot_match(route, experts, capacity):
    layers, tokens = route.shape
    span = layers * capacity
    upto = (
        lax.broadcasted_iota(jnp.int32, (tokens, tokens), 0)
        <= lax.broadcasted_iota(jnp.int32, (tokens, tokens), 1)
    ).astype(jnp.bfloat16)
    numbers = lax.broadcasted_iota(jnp.int32, (experts, tokens), 0)
    keys = []
    for layer in range(layers):
        row = route[layer : layer + 1, :]
        onehot = (numbers == row).astype(jnp.float32)
        ranks = jnp.dot(onehot.astype(jnp.bfloat16), upto, preferred_element_type=jnp.float32)
        rank = jnp.sum(onehot * ranks, axis=0, keepdims=True).astype(jnp.int32) - 1
        key = row * span + layer * capacity + rank
        keys.append(jnp.where(rank < capacity, key, -1))
    key = jnp.concatenate(keys, axis=1)
    slots = lax.broadcasted_iota(jnp.int32, (experts * span, layers * tokens), 0)
    return slots == key


def pack_kernel(
    x_hbm, dy_hbm, gate_hbm, route_hbm, out_hbm,
    x_ref, dy_ref, gate_ref, route_ref, out_ref, sems, out_sems, *, capacity
):
    layers, tokens, width = x_ref.shape
    rows = out_ref.shape[0]
    experts = rows // (layers * capacity)
    halves = (slice(0, width // 2), slice(width // 2, width))
    moves = [(route_hbm, route_ref), (gate_hbm, gate_ref)]
    for src, dst in ((x_hbm, x_ref), (dy_hbm, dy_ref)):
        moves += [(src.at[:, :, half], dst.at[:, :, half]) for half in halves]
    copies = [pltpu.make_async_copy(src, dst, sems.at[i]) for i, (src, dst) in enumerate(moves)]
    for copy in copies:
        copy.start()
    copies[0].wait()
    match = slot_match(route_ref[...], experts, capacity).astype(jnp.bfloat16)
    copies[1].wait()
    scale = jnp.concatenate([gate_ref[layer : layer + 1, :] for layer in range(layers)], axis=1)
    leaving = []
    for i, (src, table) in enumerate(((x_ref, match), (dy_ref, match * scale))):
        for j, half in enumerate(halves):
            copies[2 + 2 * i + j].wait()
            got = jnp.dot(
                table,
                src[:, :, half].reshape(layers * tokens, width // 2),
                preferred_element_type=jnp.float32,
            )
            at = slice(i * width + j * (width // 2), i * width + (j + 1) * (width // 2))
            out_ref[:, at] = got.astype(jnp.bfloat16)
            leaving.append(
                pltpu.make_async_copy(out_ref.at[:, at], out_hbm.at[:, at], out_sems.at[2 * i + j])
            )
            leaving[-1].start()
    for copy in leaving:
        copy.wait()


def fixed(shape):
    return pl.BlockSpec(shape, lambda t: (0,) * len(shape))


def pack(x, dy, gates, route, experts, capacity):
    layers, tokens, width = x.shape
    rows = experts * layers * capacity
    return pl.pallas_call(
        functools.partial(pack_kernel, capacity=capacity),
        out_shape=pltpu.HBM((rows, 2 * width), jnp.bfloat16),
        in_specs=[whole(pl.ANY)] * 4,
        out_specs=whole(pl.ANY),
        scratch_shapes=[
            pltpu.VMEM(x.shape, x.dtype),
            pltpu.VMEM(dy.shape, dy.dtype),
            pltpu.VMEM(gates.shape, gates.dtype),
            pltpu.VMEM(route.shape, route.dtype),
            pltpu.VMEM((rows, 2 * width), jnp.bfloat16),
            pltpu.SemaphoreType.DMA((6,)),
            pltpu.SemaphoreType.DMA((4,)),
        ],
        compiler_params=pltpu.CompilerParams(vmem_limit_bytes=PACK_LIMIT),
        cost_estimate=cost(2 * rows * layers * tokens * 2 * width, 5 * MIB),
        name="pack",
    )(x, dy, gates, route)


def join_kernel(gate_hbm, up_hbm, down_hbm, out_ref, down_ref, sems):
    unit = gate_hbm.shape[1]
    moves = (
        (down_hbm, down_ref),
        (gate_hbm, out_ref.at[:, :unit]),
        (up_hbm, out_ref.at[:, unit : 2 * unit]),
    )
    copies = [pltpu.make_async_copy(src, dst, sems.at[i]) for i, (src, dst) in enumerate(moves)]
    for copy in copies:
        copy.start()
    copies[0].wait()
    out_ref[:, 2 * unit :] = down_ref[...].T
    for copy in copies[1:]:
        copy.wait()


def join(w_gate, w_up, w_down):
    piece, unit = w_gate.shape
    return pl.pallas_call(
        join_kernel,
        out_shape=jax.ShapeDtypeStruct((piece, 3 * unit), jnp.bfloat16),
        in_specs=[whole(pl.ANY)] * 3,
        out_specs=whole(),
        scratch_shapes=[pltpu.VMEM(w_down.shape, w_down.dtype), pltpu.SemaphoreType.DMA((3,))],
        compiler_params=pltpu.CompilerParams(vmem_limit_bytes=JOIN_LIMIT),
        cost_estimate=cost(0, MIB),
        name="join",
    )(w_gate, w_up, w_down)


def order_kernel(place_ref, *refs):
    count = len(refs) - 2
    out_hbm, sems = refs[count], refs[count + 1]
    copies = [
        pltpu.make_async_copy(refs[i], out_hbm.at[lax.rem(place_ref[0] + i, count)], sems.at[i])
        for i in range(count)
    ]
    for copy in copies:
        copy.start()
    for copy in copies:
        copy.wait()


def order(place, blocks):
    shape = (len(blocks),) + blocks[0].shape
    return pl.pallas_call(
        order_kernel,
        out_shape=pltpu.HBM(shape, blocks[0].dtype),
        in_specs=[whole(pltpu.SMEM)] + [whole(pl.ANY)] * len(blocks),
        out_specs=whole(pl.ANY),
        scratch_shapes=[pltpu.SemaphoreType.DMA((len(blocks),))],
        compiler_params=pltpu.CompilerParams(vmem_limit_bytes=JOIN_LIMIT),
        cost_estimate=cost(0, 6 * MIB),
        name="order",
    )(place, *blocks)


def ring_gather(block):
    count = lax.axis_size("y")
    place = lax.axis_index("y").astype(jnp.int32).reshape(1)
    up = [(j, (j + 1) % count) for j in range(count)]
    down = [(j, (j - 1) % count) for j in range(count)]
    blocks = [block] * count
    fromdown = fromup = block
    for step in range(1, count // 2 + 1):
        fromdown = lax.ppermute(fromdown, "y", up)
        blocks[count - step] = fromdown
        if step < count - count // 2:
            fromup = lax.ppermute(fromup, "y", down)
            blocks[step] = fromup
    return order(place, blocks)


def forward_kernel(
    core_ref, recv_ref, own_hbm, other_hbm, grads_ref, hidden_ref, gate_ref, term_ref, held_ref, sems
):
    count, piece, columns = own_hbm.shape
    width = 2 * count * piece
    unit = columns // 6
    pieces = []
    for part in range(2):
        base = part * 3 * unit
        pieces += [slice(base, base + 2 * unit), slice(base + 2 * unit, base + 3 * unit)]
    copies = []
    for part in range(2):
        at = slice(3 * part * unit, 3 * (part + 1) * unit)
        for side, src in enumerate((own_hbm, other_hbm)):
            copies.append(
                pltpu.make_async_copy(
                    src.at[:, :, at],
                    held_ref.at[:, lax.rem(core_ref[0] + side, 2), :, at],
                    sems.at[2 * part + side],
                )
            )
    for copy in copies:
        copy.start()
    gate_sum = 0.0
    for part in range(2):
        copies[2 * part].wait()
        copies[2 * part + 1].wait()
        pre = jnp.dot(
            recv_ref[:, :width],
            held_ref[:, :, :, pieces[2 * part]].reshape(width, 2 * unit),
            preferred_element_type=jnp.float32,
        )
        back = jnp.dot(
            recv_ref[:, width:],
            held_ref[:, :, :, pieces[2 * part + 1]].reshape(width, unit),
            preferred_element_type=jnp.float32,
        )
        gate_pre, up_value = pre[:, :unit], pre[:, unit:]
        sigmoid = jax.nn.sigmoid(gate_pre)
        swish = gate_pre * sigmoid
        hidden = swish * up_value
        gate_sum = gate_sum + jnp.sum(hidden * back, axis=1, keepdims=True)
        grad_pre = back * up_value * sigmoid * (1.0 + gate_pre * (1.0 - sigmoid))
        grads_ref[:, 2 * part * unit : (2 * part + 1) * unit] = grad_pre.astype(jnp.bfloat16)
        grads_ref[:, (2 * part + 1) * unit : (2 * part + 2) * unit] = (back * swish).astype(
            jnp.bfloat16
        )
        hidden_ref[:, part * unit : (part + 1) * unit] = hidden.astype(jnp.bfloat16)
    gate_ref[...] = jnp.broadcast_to(gate_sum, gate_ref.shape).astype(jnp.bfloat16)
    weight_terms(recv_ref, grads_ref, hidden_ref, 1 - core_ref[0], term_ref)


def weight_terms(recv_ref, grads_ref, hidden_ref, side, out_ref):
    half, columns = out_ref.shape
    unit = columns // 6
    piece = 128
    blocks = min(4, half // piece)

    for at in range(0, half // piece, blocks):
        rows = slice(at * piece, (at + blocks) * piece)

        def pick(offset):
            starts = [
                pl.multiple_of(offset + (2 * (at + j) + side) * piece, piece) for j in range(blocks)
            ]
            return jnp.concatenate([recv_ref[:, pl.ds(start, piece)] for start in starts], axis=1)

        up = lax.dot_general(
            pick(0), grads_ref[...], CONTRACT_ROWS, preferred_element_type=jnp.float32
        )
        down = lax.dot_general(
            pick(2 * half), hidden_ref[...], CONTRACT_ROWS, preferred_element_type=jnp.float32
        )
        for part in range(2):
            base = part * 3 * unit
            out_ref[rows, base : base + 2 * unit] = up[
                :, 2 * part * unit : (2 * part + 2) * unit
            ].astype(out_ref.dtype)
            out_ref[rows, base + 2 * unit : base + 3 * unit] = down[
                :, part * unit : (part + 1) * unit
            ].astype(out_ref.dtype)


def forward(core, recv, own, other):
    rows = recv.shape[0]
    count, piece, columns = own.shape
    width = 2 * count * piece
    return pl.pallas_call(
        forward_kernel,
        out_shape=(
            jax.ShapeDtypeStruct((rows, columns // 6 * 4), jnp.bfloat16),
            jax.ShapeDtypeStruct((rows, columns // 3), jnp.bfloat16),
            jax.ShapeDtypeStruct((rows, 128), jnp.bfloat16),
            jax.ShapeDtypeStruct((width // 2, columns), jnp.bfloat16),
            pltpu.VMEM((count, 2, piece, columns), own.dtype),
        ),
        in_specs=[whole(pltpu.SMEM), whole(), whole(pl.ANY), whole(pl.ANY)],
        out_specs=(whole(),) * 5,
        scratch_shapes=[pltpu.SemaphoreType.DMA((4,))],
        compiler_params=pltpu.CompilerParams(vmem_limit_bytes=FORWARD_LIMIT),
        cost_estimate=cost(3 * rows * width * columns, 14 << 20),
        name="forward",
    )(core, recv, own, other)


def input_kernel(grads_ref, held_ref, gate_ref, out_ref):
    count, _, piece, columns = held_ref.shape
    unit = columns // 6
    width = 2 * count * piece
    chunk = width // 2
    for at in range(2):
        blocks = slice(at * count // 2, (at + 1) * count // 2)
        got = 0.0
        for part in range(2):
            got = got + lax.dot_general(
                grads_ref[:, 2 * part * unit : (2 * part + 2) * unit],
                held_ref[blocks, :, :, 3 * part * unit : (3 * part + 2) * unit].reshape(
                    chunk, 2 * unit
                ),
                CONTRACT_COLS,
                preferred_element_type=jnp.float32,
            )
        out_ref[:, at * chunk : (at + 1) * chunk] = got.astype(jnp.bfloat16)
    out_ref[:, width:] = gate_ref[...]


def input_terms(grads, weights, gate):
    rows = grads.shape[0]
    count, _, piece, columns = weights.shape
    width = 2 * count * piece
    return pl.pallas_call(
        input_kernel,
        out_shape=jax.ShapeDtypeStruct((rows, width + gate.shape[1]), jnp.bfloat16),
        in_specs=[whole()] * 3,
        out_specs=whole(),
        compiler_params=pltpu.CompilerParams(vmem_limit_bytes=20 * MIB),
        cost_estimate=cost(4 * rows * width * columns // 3, 9 << 20),
        name="input_terms",
    )(grads, weights, gate)


def own_kernel(core_ref, recv_ref, grads_ref, hidden_ref, out_ref):
    weight_terms(recv_ref, grads_ref, hidden_ref, core_ref[0], out_ref)


def own_terms(core, recv, grads, hidden, columns):
    rows, width = recv.shape
    return pl.pallas_call(
        own_kernel,
        out_shape=jax.ShapeDtypeStruct((width // 4, columns), jnp.float32),
        in_specs=[whole(pltpu.SMEM)] + [whole()] * 3,
        out_specs=whole(),
        compiler_params=pltpu.CompilerParams(vmem_limit_bytes=20 * MIB),
        cost_estimate=cost(rows * width * columns // 2, 10 * MIB),
        name="own_terms",
    )(core, recv, grads, hidden)


def add_kernel(own_ref, arrived_ref, out_hbm, out_ref, sems):
    count = sems.shape[0]
    rows = out_ref.shape[0] // count
    copies = []
    for i in range(count):
        at = slice(i * rows, (i + 1) * rows)
        total = own_ref[at, :] + arrived_ref[at, :].astype(jnp.float32)
        out_ref[at, :] = total.astype(jnp.bfloat16)
        copies.append(pltpu.make_async_copy(out_ref.at[at], out_hbm.at[at], sems.at[i]))
        copies[-1].start()
    for copy in copies:
        copy.wait()


def add(own, arrived):
    return pl.pallas_call(
        add_kernel,
        out_shape=pltpu.HBM(arrived.shape, jnp.bfloat16),
        in_specs=[whole()] * 2,
        out_specs=whole(pl.ANY),
        scratch_shapes=[pltpu.VMEM(arrived.shape, jnp.bfloat16), pltpu.SemaphoreType.DMA((4,))],
        compiler_params=pltpu.CompilerParams(vmem_limit_bytes=20 * MIB),
        cost_estimate=cost(arrived.size, 12 * MIB),
        name="add",
    )(own, arrived)


def unpack_kernel(back_ref, sum_ref, gate_ref, route_ref, out_ref, gate_out_ref, table_ref, *, capacity):
    layers, tokens = route_ref.shape
    experts = back_ref.shape[0] // (layers * capacity)

    @pl.when(pl.program_id(0) == 0)
    def _():
        match = slot_match(route_ref[...], experts, capacity)
        table_ref[...] = match.astype(jnp.bfloat16)
        sums = sum_ref[:, 0:1].astype(jnp.float32)
        picked = jnp.sum(jnp.where(match, sums, 0.0), axis=0, keepdims=True)
        for layer in range(layers):
            gate = gate_ref[layer : layer + 1, :].astype(jnp.float32)
            value = picked[:, layer * tokens : (layer + 1) * tokens] / gate
            gate_out_ref[layer : layer + 1, :] = value.astype(jnp.bfloat16)

    got = lax.dot_general(
        table_ref[...], back_ref[...], CONTRACT_ROWS, preferred_element_type=jnp.float32
    ).astype(jnp.bfloat16)
    out_ref[...] = got.reshape(out_ref.shape)


def unpack(back, gates, route, capacity):
    rows, columns = back.shape
    layers, tokens = route.shape
    width = columns - 128
    steps = 4
    block = width // steps
    return pl.pallas_call(
        functools.partial(unpack_kernel, capacity=capacity),
        grid=(steps,),
        out_shape=(
            jax.ShapeDtypeStruct((layers, tokens, width), jnp.bfloat16),
            jax.ShapeDtypeStruct((layers, tokens), jnp.bfloat16),
        ),
        in_specs=[
            pl.BlockSpec((rows, block), lambda t: (0, t)),
            pl.BlockSpec((rows, 128), lambda t: (0, width // 128)),
            fixed(gates.shape),
            fixed(route.shape),
        ],
        out_specs=(
            pl.BlockSpec((layers, tokens, block), lambda t: (0, 0, t)),
            fixed((layers, tokens)),
        ),
        scratch_shapes=[pltpu.VMEM((rows, layers * tokens), jnp.bfloat16)],
        compiler_params=pltpu.CompilerParams(vmem_limit_bytes=12 * MIB),
        cost_estimate=cost(2 * rows * layers * tokens * width, 3 << 20),
        name="unpack",
    )(back, back, gates, route)


def finish_kernel(reduced_ref, partner_ref, gate_ref, up_ref, down_ref):
    unit = gate_ref.shape[1]
    for i, ref in enumerate((gate_ref, up_ref, down_ref)):
        at = slice(i * unit, (i + 1) * unit)
        value = reduced_ref[:, at].astype(jnp.float32) + partner_ref[:, at].astype(jnp.float32)
        ref[...] = value if i < 2 else value.T


def finish(reduced, partner):
    piece, columns = partner.shape
    unit = columns // 3
    return pl.pallas_call(
        finish_kernel,
        out_shape=(
            jax.ShapeDtypeStruct((piece, unit), jnp.float32),
            jax.ShapeDtypeStruct((piece, unit), jnp.float32),
            jax.ShapeDtypeStruct((unit, piece), jnp.float32),
        ),
        in_specs=[pl.BlockSpec((piece, columns), lambda t: (0, 0))] * 2,
        out_specs=(fixed((piece, unit)), fixed((piece, unit)), fixed((unit, piece))),
        grid=(1,),
        compiler_params=pltpu.CompilerParams(vmem_limit_bytes=50 * MIB),
        cost_estimate=cost(piece * columns, MIB),
        name="finish",
    )(reduced, partner)


def local(inputs, cotangents, gates, routing, w_gate, w_up, w_down):
    experts = lax.axis_size("e")
    layers, tokens, width = inputs.shape
    capacity = 3 * tokens // (2 * experts)
    unit = w_gate.shape[1]
    route = routing[:, :, 0]
    core = lax.axis_index("c").astype(jnp.int32).reshape(1)
    swap = [(0, 1), (1, 0)]

    sent = pack(inputs, cotangents, gates, route, experts, capacity)
    sent, w_gate = lax.optimization_barrier((sent, w_gate))
    mine = join(w_gate, w_up, w_down)
    paired = lax.ppermute(mine, "k", swap)
    recv = lax.all_to_all(
        sent.reshape(experts, layers * capacity, 2 * width), "e", 0, 0, tiled=True
    ).reshape(experts * layers * capacity, 2 * width)
    own = ring_gather(jnp.concatenate([mine, paired], axis=1))
    other = lax.ppermute(own, "c", swap)

    grads, hidden, gate_sum, term, held = forward(core, recv, own, other)
    arrived = lax.ppermute(term, "c", swap)
    back = input_terms(grads, held, gate_sum)
    hidden, back = lax.optimization_barrier((hidden, back))
    total = own_terms(core, recv, grads, hidden, own.shape[2])
    total = add(total, arrived)
    reduced = lax.psum_scatter(total, "y", scatter_dimension=0, tiled=True)
    back = lax.all_to_all(
        back.reshape(experts, layers * capacity, back.shape[1]), "e", 0, 0, tiled=True
    ).reshape(back.shape)
    grad_inputs, grad_gates = unpack(back, gates, route, capacity)
    partner = lax.ppermute(reduced[:, 3 * unit :], "k", swap)
    return (grad_inputs, grad_gates, *finish(reduced, partner))


def solution(mesh):
    count, peers = mesh.devices.shape
    fine = Mesh(mesh.devices.reshape(count // 2, 2, peers // 2, 2), ("y", "c", "e", "k"))
    dp, expert, both = ("y", "c"), ("e", "k"), ("y", "c", "e", "k")
    return jax.shard_map(
        local,
        mesh=fine,
        in_specs=(
            P(None, both, None),
            P(None, both, None),
            P(None, both),
            P(None, both, None),
            P(dp, expert),
            P(dp, expert),
            P(expert, dp),
        ),
        out_specs=(
            P(None, both, None),
            P(None, both),
            P(dp, expert),
            P(dp, expert),
            P(expert, dp),
        ),
        check_vma=False,
    )
```

```python
import functools

import jax
import jax.numpy as jnp
from jax import lax
from jax.experimental import pallas as pl
from jax.experimental.pallas import tpu as pltpu
from jax.sharding import Mesh
from jax.sharding import PartitionSpec as P

MIB = 1024 * 1024
PACK_LIMIT = 56 * MIB
FORWARD_LIMIT = 38 * MIB
JOIN_LIMIT = 60 * MIB
CONTRACT_ROWS = (((0,), (0,)), ((), ()))
CONTRACT_COLS = (((1,), (1,)), ((), ()))


def whole(memory_space=pltpu.VMEM):
    return pl.BlockSpec(memory_space=memory_space)


def cost(flops, moved):
    return pl.CostEstimate(flops=flops, bytes_accessed=moved, transcendentals=0)


def slot_match(route, experts, capacity):
    layers, tokens = route.shape
    span = layers * capacity
    upto = (
        lax.broadcasted_iota(jnp.int32, (tokens, tokens), 0)
        <= lax.broadcasted_iota(jnp.int32, (tokens, tokens), 1)
    ).astype(jnp.bfloat16)
    numbers = lax.broadcasted_iota(jnp.int32, (experts, tokens), 0)
    keys = []
    for layer in range(layers):
        row = route[layer : layer + 1, :]
        onehot = (numbers == row).astype(jnp.float32)
        ranks = jnp.dot(onehot.astype(jnp.bfloat16), upto, preferred_element_type=jnp.float32)
        rank = jnp.sum(onehot * ranks, axis=0, keepdims=True).astype(jnp.int32) - 1
        key = row * span + layer * capacity + rank
        keys.append(jnp.where(rank < capacity, key, -1))
    key = jnp.concatenate(keys, axis=1)
    slots = lax.broadcasted_iota(jnp.int32, (experts * span, layers * tokens), 0)
    return slots == key


def pack_kernel(
    x_hbm, dy_hbm, gate_hbm, route_hbm, out_hbm,
    x_ref, dy_ref, gate_ref, route_ref, out_ref, sems, out_sems, *, capacity
):
    layers, tokens, width = x_ref.shape
    rows = out_ref.shape[0]
    experts = rows // (layers * capacity)
    halves = (slice(0, width // 2), slice(width // 2, width))
    moves = [(route_hbm, route_ref), (gate_hbm, gate_ref)]
    for src, dst in ((x_hbm, x_ref), (dy_hbm, dy_ref)):
        moves += [(src.at[:, :, half], dst.at[:, :, half]) for half in halves]
    copies = [pltpu.make_async_copy(src, dst, sems.at[i]) for i, (src, dst) in enumerate(moves)]
    for copy in copies:
        copy.start()
    copies[0].wait()
    match = slot_match(route_ref[...], experts, capacity).astype(jnp.bfloat16)
    copies[1].wait()
    scale = jnp.concatenate([gate_ref[layer : layer + 1, :] for layer in range(layers)], axis=1)
    leaving = []
    for i, (src, table) in enumerate(((x_ref, match), (dy_ref, match * scale))):
        for j, half in enumerate(halves):
            copies[2 + 2 * i + j].wait()
            got = jnp.dot(
                table,
                src[:, :, half].reshape(layers * tokens, width // 2),
                preferred_element_type=jnp.float32,
            )
            at = slice(i * width + j * (width // 2), i * width + (j + 1) * (width // 2))
            out_ref[:, at] = got.astype(jnp.bfloat16)
            leaving.append(
                pltpu.make_async_copy(out_ref.at[:, at], out_hbm.at[:, at], out_sems.at[2 * i + j])
            )
            leaving[-1].start()
    for copy in leaving:
        copy.wait()


def fixed(shape):
    return pl.BlockSpec(shape, lambda t: (0,) * len(shape))


def pack(x, dy, gates, route, experts, capacity):
    layers, tokens, width = x.shape
    rows = experts * layers * capacity
    return pl.pallas_call(
        functools.partial(pack_kernel, capacity=capacity),
        out_shape=pltpu.HBM((rows, 2 * width), jnp.bfloat16),
        in_specs=[whole(pl.ANY)] * 4,
        out_specs=whole(pl.ANY),
        scratch_shapes=[
            pltpu.VMEM(x.shape, x.dtype),
            pltpu.VMEM(dy.shape, dy.dtype),
            pltpu.VMEM(gates.shape, gates.dtype),
            pltpu.VMEM(route.shape, route.dtype),
            pltpu.VMEM((rows, 2 * width), jnp.bfloat16),
            pltpu.SemaphoreType.DMA((6,)),
            pltpu.SemaphoreType.DMA((4,)),
        ],
        compiler_params=pltpu.CompilerParams(vmem_limit_bytes=PACK_LIMIT),
        cost_estimate=cost(2 * rows * layers * tokens * 2 * width, 5 * MIB),
        name="pack",
    )(x, dy, gates, route)


def join_kernel(gate_hbm, up_hbm, down_hbm, out_ref, down_ref, sems):
    unit = gate_hbm.shape[1]
    moves = (
        (down_hbm, down_ref),
        (gate_hbm, out_ref.at[:, :unit]),
        (up_hbm, out_ref.at[:, unit : 2 * unit]),
    )
    copies = [pltpu.make_async_copy(src, dst, sems.at[i]) for i, (src, dst) in enumerate(moves)]
    for copy in copies:
        copy.start()
    copies[0].wait()
    out_ref[:, 2 * unit :] = down_ref[...].T
    for copy in copies[1:]:
        copy.wait()


def join(w_gate, w_up, w_down):
    piece, unit = w_gate.shape
    return pl.pallas_call(
        join_kernel,
        out_shape=jax.ShapeDtypeStruct((piece, 3 * unit), jnp.bfloat16),
        in_specs=[whole(pl.ANY)] * 3,
        out_specs=whole(),
        scratch_shapes=[pltpu.VMEM(w_down.shape, w_down.dtype), pltpu.SemaphoreType.DMA((3,))],
        compiler_params=pltpu.CompilerParams(vmem_limit_bytes=JOIN_LIMIT),
        cost_estimate=cost(0, MIB),
        name="join",
    )(w_gate, w_up, w_down)


def order_kernel(place_ref, *refs):
    count = len(refs) - 2
    out_ref, sems = refs[count], refs[count + 1]
    copies = [
        pltpu.make_async_copy(refs[i], out_ref.at[lax.rem(place_ref[0] + i, count)], sems.at[i])
        for i in range(count)
    ]
    for copy in copies:
        copy.start()
    for copy in copies:
        copy.wait()


def order(place, blocks):
    shape = (len(blocks),) + blocks[0].shape
    return pl.pallas_call(
        order_kernel,
        out_shape=pltpu.HBM(shape, blocks[0].dtype),
        in_specs=[whole(pltpu.SMEM)] + [whole(pl.ANY)] * len(blocks),
        out_specs=whole(),
        scratch_shapes=[pltpu.SemaphoreType.DMA((len(blocks),))],
        compiler_params=pltpu.CompilerParams(vmem_limit_bytes=JOIN_LIMIT),
        cost_estimate=cost(0, 6 * MIB),
        name="order",
    )(place, *blocks)


def ring_gather(block):
    count = lax.axis_size("y")
    place = lax.axis_index("y").astype(jnp.int32).reshape(1)
    up = [(j, (j + 1) % count) for j in range(count)]
    down = [(j, (j - 1) % count) for j in range(count)]
    blocks = [block] * count
    fromdown = fromup = block
    for step in range(1, count // 2 + 1):
        fromdown = lax.ppermute(fromdown, "y", up)
        blocks[count - step] = fromdown
        if step < count - count // 2:
            fromup = lax.ppermute(fromup, "y", down)
            blocks[step] = fromup
    return order(place, blocks)


def forward_kernel(
    core_ref, recv_ref, own_hbm, other_hbm, grads_ref, hidden_ref, gate_ref, term_ref, held_ref, sems
):
    count, piece, columns = own_hbm.shape
    width = 2 * count * piece
    unit = columns // 6
    pieces = []
    for part in range(2):
        base = part * 3 * unit
        pieces += [slice(base, base + 2 * unit), slice(base + 2 * unit, base + 3 * unit)]
    copies = []
    for part in range(2):
        at = slice(3 * part * unit, 3 * (part + 1) * unit)
        for side, src in enumerate((own_hbm, other_hbm)):
            copies.append(
                pltpu.make_async_copy(
                    src.at[:, :, at],
                    held_ref.at[:, lax.rem(core_ref[0] + side, 2), :, at],
                    sems.at[2 * part + side],
                )
            )
    for copy in copies:
        copy.start()
    gate_sum = 0.0
    for part in range(2):
        copies[2 * part].wait()
        copies[2 * part + 1].wait()
        pre = jnp.dot(
            recv_ref[:, :width],
            held_ref[:, :, :, pieces[2 * part]].reshape(width, 2 * unit),
            preferred_element_type=jnp.float32,
        )
        back = jnp.dot(
            recv_ref[:, width:],
            held_ref[:, :, :, pieces[2 * part + 1]].reshape(width, unit),
            preferred_element_type=jnp.float32,
        )
        gate_pre, up_value = pre[:, :unit], pre[:, unit:]
        sigmoid = jax.nn.sigmoid(gate_pre)
        swish = gate_pre * sigmoid
        hidden = swish * up_value
        gate_sum = gate_sum + jnp.sum(hidden * back, axis=1, keepdims=True)
        grad_pre = back * up_value * sigmoid * (1.0 + gate_pre * (1.0 - sigmoid))
        grads_ref[:, 2 * part * unit : (2 * part + 1) * unit] = grad_pre.astype(jnp.bfloat16)
        grads_ref[:, (2 * part + 1) * unit : (2 * part + 2) * unit] = (back * swish).astype(
            jnp.bfloat16
        )
        hidden_ref[:, part * unit : (part + 1) * unit] = hidden.astype(jnp.bfloat16)
    gate_ref[...] = jnp.broadcast_to(gate_sum, gate_ref.shape).astype(jnp.bfloat16)
    weight_terms(recv_ref, grads_ref, hidden_ref, 1 - core_ref[0], term_ref)


def weight_terms(recv_ref, grads_ref, hidden_ref, side, out_ref):
    half, columns = out_ref.shape
    unit = columns // 6
    piece = 128
    blocks = min(4, half // piece)

    for at in range(0, half // piece, blocks):
        rows = slice(at * piece, (at + blocks) * piece)

        def pick(offset):
            starts = [
                pl.multiple_of(offset + (2 * (at + j) + side) * piece, piece) for j in range(blocks)
            ]
            return jnp.concatenate([recv_ref[:, pl.ds(start, piece)] for start in starts], axis=1)

        up = lax.dot_general(
            pick(0), grads_ref[...], CONTRACT_ROWS, preferred_element_type=jnp.float32
        )
        down = lax.dot_general(
            pick(2 * half), hidden_ref[...], CONTRACT_ROWS, preferred_element_type=jnp.float32
        )
        for part in range(2):
            base = part * 3 * unit
            out_ref[rows, base : base + 2 * unit] = up[
                :, 2 * part * unit : (2 * part + 2) * unit
            ].astype(out_ref.dtype)
            out_ref[rows, base + 2 * unit : base + 3 * unit] = down[
                :, part * unit : (part + 1) * unit
            ].astype(out_ref.dtype)


def forward(core, recv, own, other):
    rows = recv.shape[0]
    count, piece, columns = own.shape
    width = 2 * count * piece
    return pl.pallas_call(
        forward_kernel,
        out_shape=(
            jax.ShapeDtypeStruct((rows, columns // 6 * 4), jnp.bfloat16),
            jax.ShapeDtypeStruct((rows, columns // 3), jnp.bfloat16),
            jax.ShapeDtypeStruct((rows, 128), jnp.bfloat16),
            jax.ShapeDtypeStruct((width // 2, columns), jnp.bfloat16),
            pltpu.VMEM((count, 2, piece, columns), own.dtype),
        ),
        in_specs=[whole(pltpu.SMEM), whole(), whole(pl.ANY), whole(pl.ANY)],
        out_specs=(whole(),) * 5,
        scratch_shapes=[pltpu.SemaphoreType.DMA((4,))],
        compiler_params=pltpu.CompilerParams(vmem_limit_bytes=FORWARD_LIMIT),
        cost_estimate=cost(3 * rows * width * columns, 14 << 20),
        name="forward",
    )(core, recv, own, other)


def input_kernel(grads_ref, held_ref, gate_ref, out_ref):
    count, _, piece, columns = held_ref.shape
    unit = columns // 6
    width = 2 * count * piece
    chunk = width // 2
    for at in range(2):
        blocks = slice(at * count // 2, (at + 1) * count // 2)
        got = 0.0
        for part in range(2):
            got = got + lax.dot_general(
                grads_ref[:, 2 * part * unit : (2 * part + 2) * unit],
                held_ref[blocks, :, :, 3 * part * unit : (3 * part + 2) * unit].reshape(
                    chunk, 2 * unit
                ),
                CONTRACT_COLS,
                preferred_element_type=jnp.float32,
            )
        out_ref[:, at * chunk : (at + 1) * chunk] = got.astype(jnp.bfloat16)
    out_ref[:, width:] = gate_ref[...]


def input_terms(grads, weights, gate):
    rows = grads.shape[0]
    count, _, piece, columns = weights.shape
    width = 2 * count * piece
    return pl.pallas_call(
        input_kernel,
        out_shape=jax.ShapeDtypeStruct((rows, width + gate.shape[1]), jnp.bfloat16),
        in_specs=[whole()] * 3,
        out_specs=whole(),
        compiler_params=pltpu.CompilerParams(vmem_limit_bytes=20 * MIB),
        cost_estimate=cost(4 * rows * width * columns // 3, 9 << 20),
        name="input_terms",
    )(grads, weights, gate)


def own_kernel(core_ref, recv_ref, grads_ref, hidden_ref, out_ref):
    weight_terms(recv_ref, grads_ref, hidden_ref, core_ref[0], out_ref)


def own_terms(core, recv, grads, hidden, columns):
    rows, width = recv.shape
    return pl.pallas_call(
        own_kernel,
        out_shape=jax.ShapeDtypeStruct((width // 4, columns), jnp.float32),
        in_specs=[whole(pltpu.SMEM)] + [whole()] * 3,
        out_specs=whole(),
        compiler_params=pltpu.CompilerParams(vmem_limit_bytes=20 * MIB),
        cost_estimate=cost(rows * width * columns // 2, 10 * MIB),
        name="own_terms",
    )(core, recv, grads, hidden)


def add_kernel(own_ref, arrived_ref, out_hbm, out_ref, sems):
    count = sems.shape[0]
    rows = out_ref.shape[0] // count
    copies = []
    for i in range(count):
        at = slice(i * rows, (i + 1) * rows)
        total = own_ref[at, :] + arrived_ref[at, :].astype(jnp.float32)
        out_ref[at, :] = total.astype(jnp.bfloat16)
        copies.append(pltpu.make_async_copy(out_ref.at[at], out_hbm.at[at], sems.at[i]))
        copies[-1].start()
    for copy in copies:
        copy.wait()


def add(own, arrived):
    return pl.pallas_call(
        add_kernel,
        out_shape=pltpu.HBM(arrived.shape, jnp.bfloat16),
        in_specs=[whole()] * 2,
        out_specs=whole(pl.ANY),
        scratch_shapes=[pltpu.VMEM(arrived.shape, jnp.bfloat16), pltpu.SemaphoreType.DMA((4,))],
        compiler_params=pltpu.CompilerParams(vmem_limit_bytes=20 * MIB),
        cost_estimate=cost(arrived.size, 12 * MIB),
        name="add",
    )(own, arrived)


def unpack_kernel(back_ref, sum_ref, gate_ref, route_ref, out_ref, gate_out_ref, table_ref, *, capacity):
    layers, tokens = route_ref.shape
    experts = back_ref.shape[0] // (layers * capacity)

    @pl.when(pl.program_id(0) == 0)
    def _():
        match = slot_match(route_ref[...], experts, capacity)
        table_ref[...] = match.astype(jnp.bfloat16)
        sums = sum_ref[:, 0:1].astype(jnp.float32)
        picked = jnp.sum(jnp.where(match, sums, 0.0), axis=0, keepdims=True)
        for layer in range(layers):
            gate = gate_ref[layer : layer + 1, :].astype(jnp.float32)
            value = picked[:, layer * tokens : (layer + 1) * tokens] / gate
            gate_out_ref[layer : layer + 1, :] = value.astype(jnp.bfloat16)

    got = lax.dot_general(
        table_ref[...], back_ref[...], CONTRACT_ROWS, preferred_element_type=jnp.float32
    ).astype(jnp.bfloat16)
    out_ref[...] = got.reshape(out_ref.shape)


def unpack(back, gates, route, capacity):
    rows, columns = back.shape
    layers, tokens = route.shape
    width = columns - 128
    steps = 4
    block = width // steps
    return pl.pallas_call(
        functools.partial(unpack_kernel, capacity=capacity),
        grid=(steps,),
        out_shape=(
            jax.ShapeDtypeStruct((layers, tokens, width), jnp.bfloat16),
            jax.ShapeDtypeStruct((layers, tokens), jnp.bfloat16),
        ),
        in_specs=[
            pl.BlockSpec((rows, block), lambda t: (0, t)),
            pl.BlockSpec((rows, 128), lambda t: (0, width // 128)),
            fixed(gates.shape),
            fixed(route.shape),
        ],
        out_specs=(
            pl.BlockSpec((layers, tokens, block), lambda t: (0, 0, t)),
            fixed((layers, tokens)),
        ),
        scratch_shapes=[pltpu.VMEM((rows, layers * tokens), jnp.bfloat16)],
        compiler_params=pltpu.CompilerParams(vmem_limit_bytes=12 * MIB),
        cost_estimate=cost(2 * rows * layers * tokens * width, 3 << 20),
        name="unpack",
    )(back, back, gates, route)


def finish_kernel(reduced_ref, partner_ref, gate_ref, up_ref, down_ref):
    unit = gate_ref.shape[1]
    for i, ref in enumerate((gate_ref, up_ref, down_ref)):
        at = slice(i * unit, (i + 1) * unit)
        value = reduced_ref[:, at].astype(jnp.float32) + partner_ref[:, at].astype(jnp.float32)
        ref[...] = value if i < 2 else value.T


def finish(reduced, partner):
    piece, columns = partner.shape
    unit = columns // 3
    return pl.pallas_call(
        finish_kernel,
        out_shape=(
            jax.ShapeDtypeStruct((piece, unit), jnp.float32),
            jax.ShapeDtypeStruct((piece, unit), jnp.float32),
            jax.ShapeDtypeStruct((unit, piece), jnp.float32),
        ),
        in_specs=[pl.BlockSpec((piece, columns), lambda t: (0, 0))] * 2,
        out_specs=(fixed((piece, unit)), fixed((piece, unit)), fixed((unit, piece))),
        grid=(1,),
        compiler_params=pltpu.CompilerParams(vmem_limit_bytes=50 * MIB),
        cost_estimate=cost(piece * columns, MIB),
        name="finish",
    )(reduced, partner)


def local(inputs, cotangents, gates, routing, w_gate, w_up, w_down):
    experts = lax.axis_size("e")
    layers, tokens, width = inputs.shape
    capacity = 3 * tokens // (2 * experts)
    unit = w_gate.shape[1]
    route = routing[:, :, 0]
    core = lax.axis_index("c").astype(jnp.int32).reshape(1)
    swap = [(0, 1), (1, 0)]

    sent = pack(inputs, cotangents, gates, route, experts, capacity)
    sent, w_gate = lax.optimization_barrier((sent, w_gate))
    mine = join(w_gate, w_up, w_down)
    paired = lax.ppermute(mine, "k", swap)
    recv = lax.all_to_all(
        sent.reshape(experts, layers * capacity, 2 * width), "e", 0, 0, tiled=True
    ).reshape(experts * layers * capacity, 2 * width)
    own = ring_gather(jnp.concatenate([mine, paired], axis=1))
    other = lax.ppermute(own, "c", swap)

    grads, hidden, gate_sum, term, held = forward(core, recv, own, other)
    arrived = lax.ppermute(term, "c", swap)
    back = input_terms(grads, held, gate_sum)
    hidden, back = lax.optimization_barrier((hidden, back))
    total = own_terms(core, recv, grads, hidden, own.shape[2])
    total = add(total, arrived)
    reduced = lax.psum_scatter(total, "y", scatter_dimension=0, tiled=True)
    back = lax.all_to_all(
        back.reshape(experts, layers * capacity, back.shape[1]), "e", 0, 0, tiled=True
    ).reshape(back.shape)
    grad_inputs, grad_gates = unpack(back, gates, route, capacity)
    partner = lax.ppermute(reduced[:, 3 * unit :], "k", swap)
    return (grad_inputs, grad_gates, *finish(reduced, partner))


def solution(mesh):
    count, peers = mesh.devices.shape
    fine = Mesh(mesh.devices.reshape(count // 2, 2, peers // 2, 2), ("y", "c", "e", "k"))
    dp, expert, both = ("y", "c"), ("e", "k"), ("y", "c", "e", "k")
    return jax.shard_map(
        local,
        mesh=fine,
        in_specs=(
            P(None, both, None),
            P(None, both, None),
            P(None, both),
            P(None, both, None),
            P(dp, expert),
            P(dp, expert),
            P(expert, dp),
        ),
        out_specs=(
            P(None, both, None),
            P(None, both),
            P(dp, expert),
            P(dp, expert),
            P(expert, dp),
        ),
        check_vma=False,
    )
```

```python
import functools

import jax
import jax.numpy as jnp
from jax import lax
from jax.experimental import pallas as pl
from jax.experimental.pallas import tpu as pltpu
from jax.sharding import Mesh
from jax.sharding import PartitionSpec as P

MIB = 1024 * 1024
PACK_LIMIT = 56 * MIB
FORWARD_LIMIT = 38 * MIB
JOIN_LIMIT = 60 * MIB
CONTRACT_ROWS = (((0,), (0,)), ((), ()))
CONTRACT_COLS = (((1,), (1,)), ((), ()))


def whole(memory_space=pltpu.VMEM):
    return pl.BlockSpec(memory_space=memory_space)


def cost(flops, moved):
    return pl.CostEstimate(flops=flops, bytes_accessed=moved, transcendentals=0)


def slot_match(route, experts, capacity):
    layers, tokens = route.shape
    span = layers * capacity
    upto = (
        lax.broadcasted_iota(jnp.int32, (tokens, tokens), 0)
        <= lax.broadcasted_iota(jnp.int32, (tokens, tokens), 1)
    ).astype(jnp.bfloat16)
    numbers = lax.broadcasted_iota(jnp.int32, (experts, tokens), 0)
    keys = []
    for layer in range(layers):
        row = route[layer : layer + 1, :]
        onehot = (numbers == row).astype(jnp.float32)
        ranks = jnp.dot(onehot.astype(jnp.bfloat16), upto, preferred_element_type=jnp.float32)
        rank = jnp.sum(onehot * ranks, axis=0, keepdims=True).astype(jnp.int32) - 1
        key = row * span + layer * capacity + rank
        keys.append(jnp.where(rank < capacity, key, -1))
    key = jnp.concatenate(keys, axis=1)
    slots = lax.broadcasted_iota(jnp.int32, (experts * span, layers * tokens), 0)
    return slots == key


def pack_kernel(
    x_hbm, dy_hbm, gate_hbm, route_hbm, out_hbm,
    x_ref, dy_ref, gate_ref, route_ref, out_ref, sems, out_sems, *, capacity
):
    layers, tokens, width = x_ref.shape
    rows = out_ref.shape[0]
    experts = rows // (layers * capacity)
    halves = (slice(0, width // 2), slice(width // 2, width))
    moves = [(route_hbm, route_ref), (gate_hbm, gate_ref)]
    for src, dst in ((x_hbm, x_ref), (dy_hbm, dy_ref)):
        moves += [(src.at[:, :, half], dst.at[:, :, half]) for half in halves]
    copies = [pltpu.make_async_copy(src, dst, sems.at[i]) for i, (src, dst) in enumerate(moves)]
    for copy in copies:
        copy.start()
    copies[0].wait()
    match = slot_match(route_ref[...], experts, capacity).astype(jnp.bfloat16)
    copies[1].wait()
    scale = jnp.concatenate([gate_ref[layer : layer + 1, :] for layer in range(layers)], axis=1)
    leaving = []
    for i, (src, table) in enumerate(((x_ref, match), (dy_ref, match * scale))):
        for j, half in enumerate(halves):
            copies[2 + 2 * i + j].wait()
            got = jnp.dot(
                table,
                src[:, :, half].reshape(layers * tokens, width // 2),
                preferred_element_type=jnp.float32,
            )
            at = slice(i * width + j * (width // 2), i * width + (j + 1) * (width // 2))
            out_ref[:, at] = got.astype(jnp.bfloat16)
            leaving.append(
                pltpu.make_async_copy(out_ref.at[:, at], out_hbm.at[:, at], out_sems.at[2 * i + j])
            )
            leaving[-1].start()
    for copy in leaving:
        copy.wait()


def fixed(shape):
    return pl.BlockSpec(shape, lambda t: (0,) * len(shape))


def pack(x, dy, gates, route, experts, capacity):
    layers, tokens, width = x.shape
    rows = experts * layers * capacity
    return pl.pallas_call(
        functools.partial(pack_kernel, capacity=capacity),
        out_shape=pltpu.HBM((rows, 2 * width), jnp.bfloat16),
        in_specs=[whole(pl.ANY)] * 4,
        out_specs=whole(pl.ANY),
        scratch_shapes=[
            pltpu.VMEM(x.shape, x.dtype),
            pltpu.VMEM(dy.shape, dy.dtype),
            pltpu.VMEM(gates.shape, gates.dtype),
            pltpu.VMEM(route.shape, route.dtype),
            pltpu.VMEM((rows, 2 * width), jnp.bfloat16),
            pltpu.SemaphoreType.DMA((6,)),
            pltpu.SemaphoreType.DMA((4,)),
        ],
        compiler_params=pltpu.CompilerParams(vmem_limit_bytes=PACK_LIMIT),
        cost_estimate=cost(2 * rows * layers * tokens * 2 * width, 5 * MIB),
        name="pack",
    )(x, dy, gates, route)


def join_kernel(gate_hbm, up_hbm, down_hbm, out_ref, down_ref, sems):
    unit = gate_hbm.shape[1]
    moves = (
        (down_hbm, down_ref),
        (gate_hbm, out_ref.at[:, :unit]),
        (up_hbm, out_ref.at[:, unit : 2 * unit]),
    )
    copies = [pltpu.make_async_copy(src, dst, sems.at[i]) for i, (src, dst) in enumerate(moves)]
    for copy in copies:
        copy.start()
    copies[0].wait()
    out_ref[:, 2 * unit :] = down_ref[...].T
    for copy in copies[1:]:
        copy.wait()


def join(w_gate, w_up, w_down):
    piece, unit = w_gate.shape
    return pl.pallas_call(
        join_kernel,
        out_shape=jax.ShapeDtypeStruct((piece, 3 * unit), jnp.bfloat16),
        in_specs=[whole(pl.ANY)] * 3,
        out_specs=whole(),
        scratch_shapes=[pltpu.VMEM(w_down.shape, w_down.dtype), pltpu.SemaphoreType.DMA((3,))],
        compiler_params=pltpu.CompilerParams(vmem_limit_bytes=JOIN_LIMIT),
        cost_estimate=cost(0, MIB),
        name="join",
    )(w_gate, w_up, w_down)


def order_kernel(place_ref, *refs):
    count = len(refs) - 2
    out_ref, sems = refs[count], refs[count + 1]
    copies = [
        pltpu.make_async_copy(refs[i], out_ref.at[lax.rem(place_ref[0] + i, count)], sems.at[i])
        for i in range(count)
    ]
    for copy in copies:
        copy.start()
    for copy in copies:
        copy.wait()


def order(place, blocks):
    shape = (len(blocks),) + blocks[0].shape
    return pl.pallas_call(
        order_kernel,
        out_shape=pltpu.HBM(shape, blocks[0].dtype),
        in_specs=[whole(pltpu.SMEM)] + [whole(pl.ANY)] * len(blocks),
        out_specs=whole(),
        scratch_shapes=[pltpu.SemaphoreType.DMA((len(blocks),))],
        compiler_params=pltpu.CompilerParams(vmem_limit_bytes=JOIN_LIMIT),
        cost_estimate=cost(0, 6 * MIB),
        name="order",
    )(place, *blocks)


def ring_gather(block):
    count = lax.axis_size("y")
    place = lax.axis_index("y").astype(jnp.int32).reshape(1)
    up = [(j, (j + 1) % count) for j in range(count)]
    down = [(j, (j - 1) % count) for j in range(count)]
    blocks = [block] * count
    fromdown = fromup = block
    for step in range(1, count // 2 + 1):
        fromdown = lax.ppermute(fromdown, "y", up)
        blocks[count - step] = fromdown
        if step < count - count // 2:
            fromup = lax.ppermute(fromup, "y", down)
            blocks[step] = fromup
    return order(place, blocks)


def forward_kernel(
    core_ref, recv_ref, own_hbm, other_hbm, grads_ref, hidden_ref, gate_ref, term_ref, held_ref, sems
):
    count, piece, columns = own_hbm.shape
    width = 2 * count * piece
    unit = columns // 6
    def side_copies(part):
        at = pl.ds(pl.multiple_of(3 * part * unit, unit), 3 * unit)
        return [
            pltpu.make_async_copy(
                src.at[:, :, at],
                held_ref.at[:, lax.rem(core_ref[0] + side, 2), :, at],
                sems.at[2 * part + side],
            )
            for side, src in enumerate((own_hbm, other_hbm))
        ]

    for part in range(2):
        for copy in side_copies(part):
            copy.start()

    def half(part, gate_sum):
        for copy in side_copies(part):
            copy.wait()

        def weights(first, units):
            at = pl.ds(pl.multiple_of((3 * part + first) * unit, unit), units * unit)
            return held_ref[:, :, :, at].reshape(width, units * unit)

        def column(ref, first):
            return ref.at[:, pl.ds(pl.multiple_of(first * unit, unit), unit)]

        pre = jnp.dot(recv_ref[:, :width], weights(0, 2), preferred_element_type=jnp.float32)
        back = jnp.dot(recv_ref[:, width:], weights(2, 1), preferred_element_type=jnp.float32)
        gate_pre, up_value = pre[:, :unit], pre[:, unit:]
        sigmoid = jax.nn.sigmoid(gate_pre)
        swish = gate_pre * sigmoid
        hidden = swish * up_value
        grad_pre = back * up_value * sigmoid * (1.0 + gate_pre * (1.0 - sigmoid))
        column(grads_ref, 2 * part)[...] = grad_pre.astype(jnp.bfloat16)
        column(grads_ref, 2 * part + 1)[...] = (back * swish).astype(jnp.bfloat16)
        column(hidden_ref, part)[...] = hidden.astype(jnp.bfloat16)
        return gate_sum + jnp.sum(hidden * back, axis=1, keepdims=True)

    rows = recv_ref.shape[0]
    gate_sum = lax.fori_loop(0, 2, half, jnp.zeros((rows, 1), jnp.float32))
    gate_ref[...] = jnp.broadcast_to(gate_sum, gate_ref.shape).astype(jnp.bfloat16)
    weight_terms(recv_ref, grads_ref, hidden_ref, 1 - core_ref[0], term_ref)


def weight_terms(recv_ref, grads_ref, hidden_ref, side, out_ref):
    half, columns = out_ref.shape
    unit = columns // 6
    piece = 128
    blocks = min(4, half // piece)

    for at in range(0, half // piece, blocks):
        rows = slice(at * piece, (at + blocks) * piece)

        def pick(offset):
            starts = [
                pl.multiple_of(offset + (2 * (at + j) + side) * piece, piece) for j in range(blocks)
            ]
            return jnp.concatenate([recv_ref[:, pl.ds(start, piece)] for start in starts], axis=1)

        up = lax.dot_general(
            pick(0), grads_ref[...], CONTRACT_ROWS, preferred_element_type=jnp.float32
        )
        down = lax.dot_general(
            pick(2 * half), hidden_ref[...], CONTRACT_ROWS, preferred_element_type=jnp.float32
        )
        for part in range(2):
            base = part * 3 * unit
            out_ref[rows, base : base + 2 * unit] = up[
                :, 2 * part * unit : (2 * part + 2) * unit
            ].astype(out_ref.dtype)
            out_ref[rows, base + 2 * unit : base + 3 * unit] = down[
                :, part * unit : (part + 1) * unit
            ].astype(out_ref.dtype)


def forward(core, recv, own, other):
    rows = recv.shape[0]
    count, piece, columns = own.shape
    width = 2 * count * piece
    return pl.pallas_call(
        forward_kernel,
        out_shape=(
            jax.ShapeDtypeStruct((rows, columns // 6 * 4), jnp.bfloat16),
            jax.ShapeDtypeStruct((rows, columns // 3), jnp.bfloat16),
            jax.ShapeDtypeStruct((rows, 128), jnp.bfloat16),
            jax.ShapeDtypeStruct((width // 2, columns), jnp.bfloat16),
            pltpu.VMEM((count, 2, piece, columns), own.dtype),
        ),
        in_specs=[whole(pltpu.SMEM), whole(), whole(pl.ANY), whole(pl.ANY)],
        out_specs=(whole(),) * 5,
        scratch_shapes=[pltpu.SemaphoreType.DMA((4,))],
        compiler_params=pltpu.CompilerParams(vmem_limit_bytes=FORWARD_LIMIT),
        cost_estimate=cost(3 * rows * width * columns, 14 << 20),
        name="forward",
    )(core, recv, own, other)


def input_kernel(grads_ref, held_ref, gate_ref, out_ref):
    count, _, piece, columns = held_ref.shape
    unit = columns // 6
    width = 2 * count * piece
    chunk = width // 2
    for at in range(2):
        blocks = slice(at * count // 2, (at + 1) * count // 2)
        got = 0.0
        for part in range(2):
            got = got + lax.dot_general(
                grads_ref[:, 2 * part * unit : (2 * part + 2) * unit],
                held_ref[blocks, :, :, 3 * part * unit : (3 * part + 2) * unit].reshape(
                    chunk, 2 * unit
                ),
                CONTRACT_COLS,
                preferred_element_type=jnp.float32,
            )
        out_ref[:, at * chunk : (at + 1) * chunk] = got.astype(jnp.bfloat16)
    out_ref[:, width:] = gate_ref[...]


def input_terms(grads, weights, gate):
    rows = grads.shape[0]
    count, _, piece, columns = weights.shape
    width = 2 * count * piece
    return pl.pallas_call(
        input_kernel,
        out_shape=jax.ShapeDtypeStruct((rows, width + gate.shape[1]), jnp.bfloat16),
        in_specs=[whole()] * 3,
        out_specs=whole(),
        compiler_params=pltpu.CompilerParams(vmem_limit_bytes=20 * MIB),
        cost_estimate=cost(4 * rows * width * columns // 3, 9 << 20),
        name="input_terms",
    )(grads, weights, gate)


def own_kernel(core_ref, recv_ref, grads_ref, hidden_ref, out_ref):
    weight_terms(recv_ref, grads_ref, hidden_ref, core_ref[0], out_ref)


def own_terms(core, recv, grads, hidden, columns):
    rows, width = recv.shape
    return pl.pallas_call(
        own_kernel,
        out_shape=jax.ShapeDtypeStruct((width // 4, columns), jnp.float32),
        in_specs=[whole(pltpu.SMEM)] + [whole()] * 3,
        out_specs=whole(),
        compiler_params=pltpu.CompilerParams(vmem_limit_bytes=20 * MIB),
        cost_estimate=cost(rows * width * columns // 2, 10 * MIB),
        name="own_terms",
    )(core, recv, grads, hidden)


def add_kernel(own_ref, arrived_ref, out_hbm, out_ref, sems):
    count = sems.shape[0]
    rows = out_ref.shape[0] // count
    copies = []
    for i in range(count):
        at = slice(i * rows, (i + 1) * rows)
        total = own_ref[at, :] + arrived_ref[at, :].astype(jnp.float32)
        out_ref[at, :] = total.astype(jnp.bfloat16)
        copies.append(pltpu.make_async_copy(out_ref.at[at], out_hbm.at[at], sems.at[i]))
        copies[-1].start()
    for copy in copies:
        copy.wait()


def add(own, arrived):
    return pl.pallas_call(
        add_kernel,
        out_shape=pltpu.HBM(arrived.shape, jnp.bfloat16),
        in_specs=[whole()] * 2,
        out_specs=whole(pl.ANY),
        scratch_shapes=[pltpu.VMEM(arrived.shape, jnp.bfloat16), pltpu.SemaphoreType.DMA((4,))],
        compiler_params=pltpu.CompilerParams(vmem_limit_bytes=20 * MIB),
        cost_estimate=cost(arrived.size, 12 * MIB),
        name="add",
    )(own, arrived)


def unpack_kernel(back_ref, sum_ref, gate_ref, route_ref, out_ref, gate_out_ref, table_ref, *, capacity):
    layers, tokens = route_ref.shape
    experts = back_ref.shape[0] // (layers * capacity)

    @pl.when(pl.program_id(0) == 0)
    def _():
        match = slot_match(route_ref[...], experts, capacity)
        table_ref[...] = match.astype(jnp.bfloat16)
        sums = sum_ref[:, 0:1].astype(jnp.float32)
        picked = jnp.sum(jnp.where(match, sums, 0.0), axis=0, keepdims=True)
        for layer in range(layers):
            gate = gate_ref[layer : layer + 1, :].astype(jnp.float32)
            value = picked[:, layer * tokens : (layer + 1) * tokens] / gate
            gate_out_ref[layer : layer + 1, :] = value.astype(jnp.bfloat16)

    got = lax.dot_general(
        table_ref[...], back_ref[...], CONTRACT_ROWS, preferred_element_type=jnp.float32
    ).astype(jnp.bfloat16)
    out_ref[...] = got.reshape(out_ref.shape)


def unpack(back, gates, route, capacity):
    rows, columns = back.shape
    layers, tokens = route.shape
    width = columns - 128
    steps = 4
    block = width // steps
    return pl.pallas_call(
        functools.partial(unpack_kernel, capacity=capacity),
        grid=(steps,),
        out_shape=(
            jax.ShapeDtypeStruct((layers, tokens, width), jnp.bfloat16),
            jax.ShapeDtypeStruct((layers, tokens), jnp.bfloat16),
        ),
        in_specs=[
            pl.BlockSpec((rows, block), lambda t: (0, t)),
            pl.BlockSpec((rows, 128), lambda t: (0, width // 128)),
            fixed(gates.shape),
            fixed(route.shape),
        ],
        out_specs=(
            pl.BlockSpec((layers, tokens, block), lambda t: (0, 0, t)),
            fixed((layers, tokens)),
        ),
        scratch_shapes=[pltpu.VMEM((rows, layers * tokens), jnp.bfloat16)],
        compiler_params=pltpu.CompilerParams(vmem_limit_bytes=12 * MIB),
        cost_estimate=cost(2 * rows * layers * tokens * width, 3 << 20),
        name="unpack",
    )(back, back, gates, route)


def finish_kernel(reduced_ref, partner_ref, gate_ref, up_ref, down_ref):
    unit = gate_ref.shape[1]
    for i, ref in enumerate((gate_ref, up_ref, down_ref)):
        at = slice(i * unit, (i + 1) * unit)
        value = reduced_ref[:, at].astype(jnp.float32) + partner_ref[:, at].astype(jnp.float32)
        ref[...] = value if i < 2 else value.T


def finish(reduced, partner):
    piece, columns = partner.shape
    unit = columns // 3
    return pl.pallas_call(
        finish_kernel,
        out_shape=(
            jax.ShapeDtypeStruct((piece, unit), jnp.float32),
            jax.ShapeDtypeStruct((piece, unit), jnp.float32),
            jax.ShapeDtypeStruct((unit, piece), jnp.float32),
        ),
        in_specs=[pl.BlockSpec((piece, columns), lambda t: (0, 0))] * 2,
        out_specs=(fixed((piece, unit)), fixed((piece, unit)), fixed((unit, piece))),
        grid=(1,),
        compiler_params=pltpu.CompilerParams(vmem_limit_bytes=50 * MIB),
        cost_estimate=cost(piece * columns, MIB),
        name="finish",
    )(reduced, partner)


def local(inputs, cotangents, gates, routing, w_gate, w_up, w_down):
    experts = lax.axis_size("e")
    layers, tokens, width = inputs.shape
    capacity = 3 * tokens // (2 * experts)
    unit = w_gate.shape[1]
    route = routing[:, :, 0]
    core = lax.axis_index("c").astype(jnp.int32).reshape(1)
    swap = [(0, 1), (1, 0)]

    sent = pack(inputs, cotangents, gates, route, experts, capacity)
    sent, w_gate = lax.optimization_barrier((sent, w_gate))
    mine = join(w_gate, w_up, w_down)
    paired = lax.ppermute(mine, "k", swap)
    recv = lax.all_to_all(
        sent.reshape(experts, layers * capacity, 2 * width), "e", 0, 0, tiled=True
    ).reshape(experts * layers * capacity, 2 * width)
    own = ring_gather(jnp.concatenate([mine, paired], axis=1))
    other = lax.ppermute(own, "c", swap)

    grads, hidden, gate_sum, term, held = forward(core, recv, own, other)
    arrived = lax.ppermute(term, "c", swap)
    back = input_terms(grads, held, gate_sum)
    hidden, back = lax.optimization_barrier((hidden, back))
    total = own_terms(core, recv, grads, hidden, own.shape[2])
    total = add(total, arrived)
    reduced = lax.psum_scatter(total, "y", scatter_dimension=0, tiled=True)
    back = lax.all_to_all(
        back.reshape(experts, layers * capacity, back.shape[1]), "e", 0, 0, tiled=True
    ).reshape(back.shape)
    grad_inputs, grad_gates = unpack(back, gates, route, capacity)
    partner = lax.ppermute(reduced[:, 3 * unit :], "k", swap)
    return (grad_inputs, grad_gates, *finish(reduced, partner))


def solution(mesh):
    count, peers = mesh.devices.shape
    fine = Mesh(mesh.devices.reshape(count // 2, 2, peers // 2, 2), ("y", "c", "e", "k"))
    dp, expert, both = ("y", "c"), ("e", "k"), ("y", "c", "e", "k")
    return jax.shard_map(
        local,
        mesh=fine,
        in_specs=(
            P(None, both, None),
            P(None, both, None),
            P(None, both),
            P(None, both, None),
            P(dp, expert),
            P(dp, expert),
            P(expert, dp),
        ),
        out_specs=(
            P(None, both, None),
            P(None, both),
            P(dp, expert),
            P(dp, expert),
            P(expert, dp),
        ),
        check_vma=False,
    )
```

```python
import functools

import jax
import jax.numpy as jnp
from jax import lax
from jax.experimental import pallas as pl
from jax.experimental.pallas import tpu as pltpu
from jax.sharding import Mesh
from jax.sharding import PartitionSpec as P

MIB = 1024 * 1024
PACK_LIMIT = 56 * MIB
FORWARD_LIMIT = 38 * MIB
JOIN_LIMIT = 60 * MIB
CONTRACT_ROWS = (((0,), (0,)), ((), ()))
CONTRACT_COLS = (((1,), (1,)), ((), ()))


def whole(memory_space=pltpu.VMEM):
    return pl.BlockSpec(memory_space=memory_space)


def cost(flops, moved):
    return pl.CostEstimate(flops=flops, bytes_accessed=moved, transcendentals=0)


def slot_match(route, experts, capacity):
    layers, tokens = route.shape
    span = layers * capacity
    upto = (
        lax.broadcasted_iota(jnp.int32, (tokens, tokens), 0)
        <= lax.broadcasted_iota(jnp.int32, (tokens, tokens), 1)
    ).astype(jnp.bfloat16)
    numbers = lax.broadcasted_iota(jnp.int32, (experts, tokens), 0)
    keys = []
    for layer in range(layers):
        row = route[layer : layer + 1, :]
        onehot = (numbers == row).astype(jnp.float32)
        ranks = jnp.dot(onehot.astype(jnp.bfloat16), upto, preferred_element_type=jnp.float32)
        rank = jnp.sum(onehot * ranks, axis=0, keepdims=True).astype(jnp.int32) - 1
        key = row * span + layer * capacity + rank
        keys.append(jnp.where(rank < capacity, key, -1))
    key = jnp.concatenate(keys, axis=1)
    slots = lax.broadcasted_iota(jnp.int32, (experts * span, layers * tokens), 0)
    return slots == key


def pack_kernel(
    x_hbm, dy_hbm, gate_hbm, route_hbm, out_hbm,
    x_ref, dy_ref, gate_ref, route_ref, out_ref, sems, out_sems, *, capacity
):
    layers, tokens, width = x_ref.shape
    rows = out_ref.shape[0]
    experts = rows // (layers * capacity)
    halves = (slice(0, width // 2), slice(width // 2, width))
    moves = [(route_hbm, route_ref), (gate_hbm, gate_ref)]
    for src, dst in ((x_hbm, x_ref), (dy_hbm, dy_ref)):
        moves += [(src.at[:, :, half], dst.at[:, :, half]) for half in halves]
    copies = [pltpu.make_async_copy(src, dst, sems.at[i]) for i, (src, dst) in enumerate(moves)]
    for copy in copies:
        copy.start()
    copies[0].wait()
    match = slot_match(route_ref[...], experts, capacity).astype(jnp.bfloat16)
    copies[1].wait()
    scale = jnp.concatenate([gate_ref[layer : layer + 1, :] for layer in range(layers)], axis=1)
    leaving = []
    for i, (src, table) in enumerate(((x_ref, match), (dy_ref, match * scale))):
        for j, half in enumerate(halves):
            copies[2 + 2 * i + j].wait()
            got = jnp.dot(
                table,
                src[:, :, half].reshape(layers * tokens, width // 2),
                preferred_element_type=jnp.float32,
            )
            at = slice(i * width + j * (width // 2), i * width + (j + 1) * (width // 2))
            out_ref[:, at] = got.astype(jnp.bfloat16)
            leaving.append(
                pltpu.make_async_copy(out_ref.at[:, at], out_hbm.at[:, at], out_sems.at[2 * i + j])
            )
            leaving[-1].start()
    for copy in leaving:
        copy.wait()


def fixed(shape):
    return pl.BlockSpec(shape, lambda t: (0,) * len(shape))


def pack(x, dy, gates, route, experts, capacity):
    layers, tokens, width = x.shape
    rows = experts * layers * capacity
    return pl.pallas_call(
        functools.partial(pack_kernel, capacity=capacity),
        out_shape=pltpu.HBM((rows, 2 * width), jnp.bfloat16),
        in_specs=[whole(pl.ANY)] * 4,
        out_specs=whole(pl.ANY),
        scratch_shapes=[
            pltpu.VMEM(x.shape, x.dtype),
            pltpu.VMEM(dy.shape, dy.dtype),
            pltpu.VMEM(gates.shape, gates.dtype),
            pltpu.VMEM(route.shape, route.dtype),
            pltpu.VMEM((rows, 2 * width), jnp.bfloat16),
            pltpu.SemaphoreType.DMA((6,)),
            pltpu.SemaphoreType.DMA((4,)),
        ],
        compiler_params=pltpu.CompilerParams(vmem_limit_bytes=PACK_LIMIT),
        cost_estimate=cost(2 * rows * layers * tokens * 2 * width, 5 * MIB),
        name="pack",
    )(x, dy, gates, route)


def join_kernel(gate_hbm, up_hbm, down_hbm, out_ref, down_ref, sems):
    unit = gate_hbm.shape[1]
    moves = (
        (down_hbm, down_ref),
        (gate_hbm, out_ref.at[:, :unit]),
        (up_hbm, out_ref.at[:, unit : 2 * unit]),
    )
    copies = [pltpu.make_async_copy(src, dst, sems.at[i]) for i, (src, dst) in enumerate(moves)]
    for copy in copies:
        copy.start()
    copies[0].wait()
    out_ref[:, 2 * unit :] = down_ref[...].T
    for copy in copies[1:]:
        copy.wait()


def join(w_gate, w_up, w_down):
    piece, unit = w_gate.shape
    return pl.pallas_call(
        join_kernel,
        out_shape=jax.ShapeDtypeStruct((piece, 3 * unit), jnp.bfloat16),
        in_specs=[whole(pl.ANY)] * 3,
        out_specs=whole(),
        scratch_shapes=[pltpu.VMEM(w_down.shape, w_down.dtype), pltpu.SemaphoreType.DMA((3,))],
        compiler_params=pltpu.CompilerParams(vmem_limit_bytes=JOIN_LIMIT),
        cost_estimate=cost(0, MIB),
        name="join",
    )(w_gate, w_up, w_down)


def order_kernel(place_ref, *refs):
    count = len(refs) - 2
    out_ref, sems = refs[count], refs[count + 1]
    copies = [
        pltpu.make_async_copy(refs[i], out_ref.at[lax.rem(place_ref[0] + i, count)], sems.at[i])
        for i in range(count)
    ]
    for copy in copies:
        copy.start()
    for copy in copies:
        copy.wait()


def order(place, blocks):
    shape = (len(blocks),) + blocks[0].shape
    return pl.pallas_call(
        order_kernel,
        out_shape=pltpu.HBM(shape, blocks[0].dtype),
        in_specs=[whole(pltpu.SMEM)] + [whole(pl.ANY)] * len(blocks),
        out_specs=whole(),
        scratch_shapes=[pltpu.SemaphoreType.DMA((len(blocks),))],
        compiler_params=pltpu.CompilerParams(vmem_limit_bytes=JOIN_LIMIT),
        cost_estimate=cost(0, 6 * MIB),
        name="order",
    )(place, *blocks)


def ring_gather(block):
    count = lax.axis_size("y")
    place = lax.axis_index("y").astype(jnp.int32).reshape(1)
    up = [(j, (j + 1) % count) for j in range(count)]
    down = [(j, (j - 1) % count) for j in range(count)]
    blocks = [block] * count
    fromdown = fromup = block
    for step in range(1, count // 2 + 1):
        fromdown = lax.ppermute(fromdown, "y", up)
        blocks[count - step] = fromdown
        if step < count - count // 2:
            fromup = lax.ppermute(fromup, "y", down)
            blocks[step] = fromup
    return order(place, blocks)


def forward_kernel(
    core_ref, recv_ref, own_hbm, other_hbm, grads_ref, hidden_ref, gate_ref, term_ref, held_ref, sems
):
    count, piece, columns = own_hbm.shape
    width = 2 * count * piece
    unit = columns // 6
    def side_copies(part):
        at = pl.ds(pl.multiple_of(3 * part * unit, unit), 3 * unit)
        return [
            pltpu.make_async_copy(
                src.at[:, :, at],
                held_ref.at[:, lax.rem(core_ref[0] + side, 2), :, at],
                sems.at[2 * part + side],
            )
            for side, src in enumerate((own_hbm, other_hbm))
        ]

    for part in range(2):
        for copy in side_copies(part):
            copy.start()

    def half(part, gate_sum):
        for copy in side_copies(part):
            copy.wait()

        def weights(first, units):
            at = pl.ds(pl.multiple_of((3 * part + first) * unit, unit), units * unit)
            return held_ref[:, :, :, at].reshape(width, units * unit)

        def column(ref, first):
            return ref.at[:, pl.ds(pl.multiple_of(first * unit, unit), unit)]

        pre = jnp.dot(recv_ref[:, :width], weights(0, 2), preferred_element_type=jnp.float32)
        back = jnp.dot(recv_ref[:, width:], weights(2, 1), preferred_element_type=jnp.float32)
        gate_pre, up_value = pre[:, :unit], pre[:, unit:]
        sigmoid = jax.nn.sigmoid(gate_pre)
        swish = gate_pre * sigmoid
        hidden = swish * up_value
        grad_pre = back * up_value * sigmoid * (1.0 + gate_pre * (1.0 - sigmoid))
        column(grads_ref, 2 * part)[...] = grad_pre.astype(jnp.bfloat16)
        column(grads_ref, 2 * part + 1)[...] = (back * swish).astype(jnp.bfloat16)
        column(hidden_ref, part)[...] = hidden.astype(jnp.bfloat16)
        return gate_sum + jnp.sum(hidden * back, axis=1, keepdims=True)

    rows = recv_ref.shape[0]
    gate_sum = lax.fori_loop(0, 2, half, jnp.zeros((rows, 1), jnp.float32))
    gate_ref[...] = jnp.broadcast_to(gate_sum, gate_ref.shape).astype(jnp.bfloat16)
    weight_terms(recv_ref, grads_ref, hidden_ref, 1 - core_ref[0], term_ref)


def weight_terms(recv_ref, grads_ref, hidden_ref, side, out_ref):
    half, columns = out_ref.shape
    unit = columns // 6
    piece = 128
    blocks = min(4, half // piece)

    for at in range(0, half // piece, blocks):
        rows = slice(at * piece, (at + blocks) * piece)

        def pick(offset):
            starts = [
                pl.multiple_of(offset + (2 * (at + j) + side) * piece, piece) for j in range(blocks)
            ]
            return jnp.concatenate([recv_ref[:, pl.ds(start, piece)] for start in starts], axis=1)

        up = lax.dot_general(
            pick(0), grads_ref[...], CONTRACT_ROWS, preferred_element_type=jnp.float32
        )
        down = lax.dot_general(
            pick(2 * half), hidden_ref[...], CONTRACT_ROWS, preferred_element_type=jnp.float32
        )
        for part in range(2):
            base = part * 3 * unit
            out_ref[rows, base : base + 2 * unit] = up[
                :, 2 * part * unit : (2 * part + 2) * unit
            ].astype(out_ref.dtype)
            out_ref[rows, base + 2 * unit : base + 3 * unit] = down[
                :, part * unit : (part + 1) * unit
            ].astype(out_ref.dtype)


def forward(core, recv, own, other):
    rows = recv.shape[0]
    count, piece, columns = own.shape
    width = 2 * count * piece
    return pl.pallas_call(
        forward_kernel,
        out_shape=(
            jax.ShapeDtypeStruct((rows, columns // 6 * 4), jnp.bfloat16),
            jax.ShapeDtypeStruct((rows, columns // 3), jnp.bfloat16),
            jax.ShapeDtypeStruct((rows, 128), jnp.bfloat16),
            jax.ShapeDtypeStruct((width // 2, columns), jnp.bfloat16),
            pltpu.VMEM((count, 2, piece, columns), own.dtype),
        ),
        in_specs=[whole(pltpu.SMEM), whole(), whole(pl.ANY), whole(pl.ANY)],
        out_specs=(whole(),) * 5,
        scratch_shapes=[pltpu.SemaphoreType.DMA((4,))],
        compiler_params=pltpu.CompilerParams(vmem_limit_bytes=FORWARD_LIMIT),
        cost_estimate=cost(3 * rows * width * columns, 14 << 20),
        name="forward",
    )(core, recv, own, other)


def input_kernel(grads_ref, held_ref, gate_ref, out_ref):
    count, _, piece, columns = held_ref.shape
    unit = columns // 6
    width = 2 * count * piece
    chunk = width // 2
    for at in range(2):
        blocks = slice(at * count // 2, (at + 1) * count // 2)
        got = 0.0
        for part in range(2):
            got = got + lax.dot_general(
                grads_ref[:, 2 * part * unit : (2 * part + 2) * unit],
                held_ref[blocks, :, :, 3 * part * unit : (3 * part + 2) * unit].reshape(
                    chunk, 2 * unit
                ),
                CONTRACT_COLS,
                preferred_element_type=jnp.float32,
            )
        out_ref[:, at * chunk : (at + 1) * chunk] = got.astype(jnp.bfloat16)
    out_ref[:, width:] = gate_ref[...]


def input_terms(grads, weights, gate):
    rows = grads.shape[0]
    count, _, piece, columns = weights.shape
    width = 2 * count * piece
    return pl.pallas_call(
        input_kernel,
        out_shape=jax.ShapeDtypeStruct((rows, width + gate.shape[1]), jnp.bfloat16),
        in_specs=[whole()] * 3,
        out_specs=whole(),
        compiler_params=pltpu.CompilerParams(vmem_limit_bytes=20 * MIB),
        cost_estimate=cost(4 * rows * width * columns // 3, 9 << 20),
        name="input_terms",
    )(grads, weights, gate)


def own_kernel(core_ref, recv_ref, grads_ref, hidden_ref, out_ref):
    weight_terms(recv_ref, grads_ref, hidden_ref, core_ref[0], out_ref)


def own_terms(core, recv, grads, hidden, columns):
    rows, width = recv.shape
    return pl.pallas_call(
        own_kernel,
        out_shape=jax.ShapeDtypeStruct((width // 4, columns), jnp.float32),
        in_specs=[whole(pltpu.SMEM)] + [whole()] * 3,
        out_specs=whole(),
        compiler_params=pltpu.CompilerParams(vmem_limit_bytes=20 * MIB),
        cost_estimate=cost(rows * width * columns // 2, 10 * MIB),
        name="own_terms",
    )(core, recv, grads, hidden)


def add_kernel(own_ref, arrived_ref, out_hbm, out_ref, sems):
    count = sems.shape[0]
    rows, columns = own_ref.shape
    rows, columns = rows // count, columns // 2
    copies = []
    for i in range(count):
        at = slice(i * rows, (i + 1) * rows)
        for part in range(2):
            side = slice(part * columns, (part + 1) * columns)
            total = own_ref[at, side] + arrived_ref[at, side].astype(jnp.float32)
            first = (2 * i + part) * rows
            out_ref[first : first + rows, :] = total.astype(jnp.bfloat16)
        both = pl.ds(2 * i * rows, 2 * rows)
        copies.append(pltpu.make_async_copy(out_ref.at[both], out_hbm.at[both], sems.at[i]))
        copies[-1].start()
    for copy in copies:
        copy.wait()


def add(own, arrived, piece):
    rows, columns = arrived.shape
    shape = (2 * rows, columns // 2)
    return pl.pallas_call(
        add_kernel,
        out_shape=pltpu.HBM(shape, jnp.bfloat16),
        in_specs=[whole()] * 2,
        out_specs=whole(pl.ANY),
        scratch_shapes=[
            pltpu.VMEM(shape, jnp.bfloat16),
            pltpu.SemaphoreType.DMA((rows // piece,)),
        ],
        compiler_params=pltpu.CompilerParams(vmem_limit_bytes=20 * MIB),
        cost_estimate=cost(arrived.size, 12 * MIB),
        name="add",
    )(own, arrived)


def unpack_kernel(back_ref, sum_ref, gate_ref, route_ref, out_ref, gate_out_ref, table_ref, *, capacity):
    layers, tokens = route_ref.shape
    experts = back_ref.shape[0] // (layers * capacity)

    @pl.when(pl.program_id(0) == 0)
    def _():
        match = slot_match(route_ref[...], experts, capacity)
        table_ref[...] = match.astype(jnp.bfloat16)
        sums = sum_ref[:, 0:1].astype(jnp.float32)
        picked = jnp.sum(jnp.where(match, sums, 0.0), axis=0, keepdims=True)
        for layer in range(layers):
            gate = gate_ref[layer : layer + 1, :].astype(jnp.float32)
            value = picked[:, layer * tokens : (layer + 1) * tokens] / gate
            gate_out_ref[layer : layer + 1, :] = value.astype(jnp.bfloat16)

    got = lax.dot_general(
        table_ref[...], back_ref[...], CONTRACT_ROWS, preferred_element_type=jnp.float32
    ).astype(jnp.bfloat16)
    out_ref[...] = got.reshape(out_ref.shape)


def unpack(back, gates, route, capacity):
    rows, columns = back.shape
    layers, tokens = route.shape
    width = columns - 128
    steps = 4
    block = width // steps
    return pl.pallas_call(
        functools.partial(unpack_kernel, capacity=capacity),
        grid=(steps,),
        out_shape=(
            jax.ShapeDtypeStruct((layers, tokens, width), jnp.bfloat16),
            jax.ShapeDtypeStruct((layers, tokens), jnp.bfloat16),
        ),
        in_specs=[
            pl.BlockSpec((rows, block), lambda t: (0, t)),
            pl.BlockSpec((rows, 128), lambda t: (0, width // 128)),
            fixed(gates.shape),
            fixed(route.shape),
        ],
        out_specs=(
            pl.BlockSpec((layers, tokens, block), lambda t: (0, 0, t)),
            fixed((layers, tokens)),
        ),
        scratch_shapes=[pltpu.VMEM((rows, layers * tokens), jnp.bfloat16)],
        compiler_params=pltpu.CompilerParams(vmem_limit_bytes=12 * MIB),
        cost_estimate=cost(2 * rows * layers * tokens * width, 3 << 20),
        name="unpack",
    )(back, back, gates, route)


def finish_kernel(reduced_ref, partner_ref, gate_ref, up_ref, down_ref):
    unit = gate_ref.shape[1]
    for i, ref in enumerate((gate_ref, up_ref, down_ref)):
        at = slice(i * unit, (i + 1) * unit)
        value = reduced_ref[:, at].astype(jnp.float32) + partner_ref[:, at].astype(jnp.float32)
        ref[...] = value if i < 2 else value.T


def finish(reduced, partner):
    piece, columns = partner.shape
    unit = columns // 3
    return pl.pallas_call(
        finish_kernel,
        out_shape=(
            jax.ShapeDtypeStruct((piece, unit), jnp.float32),
            jax.ShapeDtypeStruct((piece, unit), jnp.float32),
            jax.ShapeDtypeStruct((unit, piece), jnp.float32),
        ),
        in_specs=[pl.BlockSpec((piece, columns), lambda t: (0, 0))] * 2,
        out_specs=(fixed((piece, unit)), fixed((piece, unit)), fixed((unit, piece))),
        grid=(1,),
        compiler_params=pltpu.CompilerParams(vmem_limit_bytes=50 * MIB),
        cost_estimate=cost(piece * columns, MIB),
        name="finish",
    )(reduced, partner)


def local(inputs, cotangents, gates, routing, w_gate, w_up, w_down):
    experts = lax.axis_size("e")
    layers, tokens, width = inputs.shape
    capacity = 3 * tokens // (2 * experts)
    unit = w_gate.shape[1]
    route = routing[:, :, 0]
    core = lax.axis_index("c").astype(jnp.int32).reshape(1)
    swap = [(0, 1), (1, 0)]

    sent = pack(inputs, cotangents, gates, route, experts, capacity)
    sent, w_gate = lax.optimization_barrier((sent, w_gate))
    mine = join(w_gate, w_up, w_down)
    paired = lax.ppermute(mine, "k", swap)
    recv = lax.all_to_all(
        sent.reshape(experts, layers * capacity, 2 * width), "e", 0, 0, tiled=True
    ).reshape(experts * layers * capacity, 2 * width)
    own = ring_gather(jnp.concatenate([mine, paired], axis=1))
    other = lax.ppermute(own, "c", swap)

    grads, hidden, gate_sum, term, held = forward(core, recv, own, other)
    arrived = lax.ppermute(term, "c", swap)
    back = input_terms(grads, held, gate_sum)
    hidden, back = lax.optimization_barrier((hidden, back))
    total = own_terms(core, recv, grads, hidden, own.shape[2])
    total = add(total, arrived, w_gate.shape[0])
    reduced = lax.psum_scatter(total, "y", scatter_dimension=0, tiled=True)
    back = lax.all_to_all(
        back.reshape(experts, layers * capacity, back.shape[1]), "e", 0, 0, tiled=True
    ).reshape(back.shape)
    grad_inputs, grad_gates = unpack(back, gates, route, capacity)
    partner = lax.ppermute(reduced[w_gate.shape[0] :], "k", swap)
    return (grad_inputs, grad_gates, *finish(reduced, partner))


def solution(mesh):
    count, peers = mesh.devices.shape
    fine = Mesh(mesh.devices.reshape(count // 2, 2, peers // 2, 2), ("y", "c", "e", "k"))
    dp, expert, both = ("y", "c"), ("e", "k"), ("y", "c", "e", "k")
    return jax.shard_map(
        local,
        mesh=fine,
        in_specs=(
            P(None, both, None),
            P(None, both, None),
            P(None, both),
            P(None, both, None),
            P(dp, expert),
            P(dp, expert),
            P(expert, dp),
        ),
        out_specs=(
            P(None, both, None),
            P(None, both),
            P(dp, expert),
            P(dp, expert),
            P(expert, dp),
        ),
        check_vma=False,
    )
```

```python
import functools

import jax
import jax.numpy as jnp
from jax import lax
from jax.experimental import pallas as pl
from jax.experimental.pallas import tpu as pltpu
from jax.sharding import Mesh
from jax.sharding import PartitionSpec as P

MIB = 1024 * 1024
PACK_LIMIT = 56 * MIB
FORWARD_LIMIT = 38 * MIB
JOIN_LIMIT = 60 * MIB
CONTRACT_ROWS = (((0,), (0,)), ((), ()))
CONTRACT_COLS = (((1,), (1,)), ((), ()))


def whole(memory_space=pltpu.VMEM):
    return pl.BlockSpec(memory_space=memory_space)


def cost(flops, moved):
    return pl.CostEstimate(flops=flops, bytes_accessed=moved, transcendentals=0)


def slot_match(route, experts, capacity):
    layers, tokens = route.shape
    span = layers * capacity
    upto = (
        lax.broadcasted_iota(jnp.int32, (tokens, tokens), 0)
        <= lax.broadcasted_iota(jnp.int32, (tokens, tokens), 1)
    ).astype(jnp.bfloat16)
    numbers = lax.broadcasted_iota(jnp.int32, (experts, tokens), 0)
    keys = []
    for layer in range(layers):
        row = route[layer : layer + 1, :]
        onehot = (numbers == row).astype(jnp.float32)
        ranks = jnp.dot(onehot.astype(jnp.bfloat16), upto, preferred_element_type=jnp.float32)
        rank = jnp.sum(onehot * ranks, axis=0, keepdims=True).astype(jnp.int32) - 1
        key = row * span + layer * capacity + rank
        keys.append(jnp.where(rank < capacity, key, -1))
    key = jnp.concatenate(keys, axis=1)
    slots = lax.broadcasted_iota(jnp.int32, (experts * span, layers * tokens), 0)
    return slots == key


def pack_kernel(
    x_hbm, dy_hbm, gate_hbm, route_hbm, out_hbm,
    x_ref, dy_ref, gate_ref, route_ref, out_ref, sems, out_sems, *, capacity
):
    layers, tokens, width = x_ref.shape
    rows = out_ref.shape[0]
    experts = rows // (layers * capacity)
    halves = (slice(0, width // 2), slice(width // 2, width))
    moves = [(route_hbm, route_ref), (gate_hbm, gate_ref)]
    for src, dst in ((x_hbm, x_ref), (dy_hbm, dy_ref)):
        moves += [(src.at[:, :, half], dst.at[:, :, half]) for half in halves]
    copies = [pltpu.make_async_copy(src, dst, sems.at[i]) for i, (src, dst) in enumerate(moves)]
    for copy in copies:
        copy.start()
    copies[0].wait()
    match = slot_match(route_ref[...], experts, capacity).astype(jnp.bfloat16)
    copies[1].wait()
    scale = jnp.concatenate([gate_ref[layer : layer + 1, :] for layer in range(layers)], axis=1)
    leaving = []
    for i, (src, table) in enumerate(((x_ref, match), (dy_ref, match * scale))):
        for j, half in enumerate(halves):
            copies[2 + 2 * i + j].wait()
            got = jnp.dot(
                table,
                src[:, :, half].reshape(layers * tokens, width // 2),
                preferred_element_type=jnp.float32,
            )
            at = slice(i * width + j * (width // 2), i * width + (j + 1) * (width // 2))
            out_ref[:, at] = got.astype(jnp.bfloat16)
            leaving.append(
                pltpu.make_async_copy(out_ref.at[:, at], out_hbm.at[:, at], out_sems.at[2 * i + j])
            )
            leaving[-1].start()
    for copy in leaving:
        copy.wait()


def fixed(shape):
    return pl.BlockSpec(shape, lambda t: (0,) * len(shape))


def pack(x, dy, gates, route, experts, capacity):
    layers, tokens, width = x.shape
    rows = experts * layers * capacity
    return pl.pallas_call(
        functools.partial(pack_kernel, capacity=capacity),
        out_shape=pltpu.HBM((rows, 2 * width), jnp.bfloat16),
        in_specs=[whole(pl.ANY)] * 4,
        out_specs=whole(pl.ANY),
        scratch_shapes=[
            pltpu.VMEM(x.shape, x.dtype),
            pltpu.VMEM(dy.shape, dy.dtype),
            pltpu.VMEM(gates.shape, gates.dtype),
            pltpu.VMEM(route.shape, route.dtype),
            pltpu.VMEM((rows, 2 * width), jnp.bfloat16),
            pltpu.SemaphoreType.DMA((6,)),
            pltpu.SemaphoreType.DMA((4,)),
        ],
        compiler_params=pltpu.CompilerParams(vmem_limit_bytes=PACK_LIMIT),
        cost_estimate=cost(2 * rows * layers * tokens * 2 * width, 5 * MIB),
        name="pack",
    )(x, dy, gates, route)


def join_kernel(gate_hbm, up_hbm, down_hbm, out_ref, down_ref, sems):
    unit = gate_hbm.shape[1]
    moves = (
        (down_hbm, down_ref),
        (gate_hbm, out_ref.at[:, :unit]),
        (up_hbm, out_ref.at[:, unit : 2 * unit]),
    )
    copies = [pltpu.make_async_copy(src, dst, sems.at[i]) for i, (src, dst) in enumerate(moves)]
    for copy in copies:
        copy.start()
    copies[0].wait()
    out_ref[:, 2 * unit :] = down_ref[...].T
    for copy in copies[1:]:
        copy.wait()


def join(w_gate, w_up, w_down):
    piece, unit = w_gate.shape
    return pl.pallas_call(
        join_kernel,
        out_shape=jax.ShapeDtypeStruct((piece, 3 * unit), jnp.bfloat16),
        in_specs=[whole(pl.ANY)] * 3,
        out_specs=whole(),
        scratch_shapes=[pltpu.VMEM(w_down.shape, w_down.dtype), pltpu.SemaphoreType.DMA((3,))],
        compiler_params=pltpu.CompilerParams(vmem_limit_bytes=JOIN_LIMIT),
        cost_estimate=cost(0, MIB),
        name="join",
    )(w_gate, w_up, w_down)


def order_kernel(place_ref, *refs):
    count = len(refs) - 2
    out_ref, sems = refs[count], refs[count + 1]
    copies = [
        pltpu.make_async_copy(refs[i], out_ref.at[lax.rem(place_ref[0] + i, count)], sems.at[i])
        for i in range(count)
    ]
    for copy in copies:
        copy.start()
    for copy in copies:
        copy.wait()


def order(place, blocks):
    shape = (len(blocks),) + blocks[0].shape
    return pl.pallas_call(
        order_kernel,
        out_shape=pltpu.HBM(shape, blocks[0].dtype),
        in_specs=[whole(pltpu.SMEM)] + [whole(pl.ANY)] * len(blocks),
        out_specs=whole(),
        scratch_shapes=[pltpu.SemaphoreType.DMA((len(blocks),))],
        compiler_params=pltpu.CompilerParams(vmem_limit_bytes=JOIN_LIMIT),
        cost_estimate=cost(0, 6 * MIB),
        name="order",
    )(place, *blocks)


def ring_gather(block):
    count = lax.axis_size("y")
    place = lax.axis_index("y").astype(jnp.int32).reshape(1)
    up = [(j, (j + 1) % count) for j in range(count)]
    down = [(j, (j - 1) % count) for j in range(count)]
    blocks = [block] * count
    fromdown = fromup = block
    for step in range(1, count // 2 + 1):
        fromdown = lax.ppermute(fromdown, "y", up)
        blocks[count - step] = fromdown
        if step < count - count // 2:
            fromup = lax.ppermute(fromup, "y", down)
            blocks[step] = fromup
    return order(place, blocks)


def forward_kernel(
    core_ref, recv_ref, own_hbm, other_hbm, grads_ref, hidden_ref, gate_ref, term_ref, held_ref, sems
):
    count, piece, columns = own_hbm.shape
    width = 2 * count * piece
    unit = columns // 6
    def side_copies(part):
        at = pl.ds(pl.multiple_of(3 * part * unit, unit), 3 * unit)
        return [
            pltpu.make_async_copy(
                src.at[:, :, at],
                held_ref.at[:, lax.rem(core_ref[0] + side, 2), :, at],
                sems.at[2 * part + side],
            )
            for side, src in enumerate((own_hbm, other_hbm))
        ]

    for part in range(2):
        for copy in side_copies(part):
            copy.start()

    def half(part, gate_sum):
        for copy in side_copies(part):
            copy.wait()

        def weights(first, units):
            at = pl.ds(pl.multiple_of((3 * part + first) * unit, unit), units * unit)
            return held_ref[:, :, :, at].reshape(width, units * unit)

        def column(ref, first):
            return ref.at[:, pl.ds(pl.multiple_of(first * unit, unit), unit)]

        pre = jnp.dot(recv_ref[:, :width], weights(0, 2), preferred_element_type=jnp.float32)
        back = jnp.dot(recv_ref[:, width:], weights(2, 1), preferred_element_type=jnp.float32)
        gate_pre, up_value = pre[:, :unit], pre[:, unit:]
        sigmoid = jax.nn.sigmoid(gate_pre)
        swish = gate_pre * sigmoid
        hidden = swish * up_value
        grad_pre = back * up_value * sigmoid * (1.0 + gate_pre * (1.0 - sigmoid))
        column(grads_ref, 2 * part)[...] = grad_pre.astype(jnp.bfloat16)
        column(grads_ref, 2 * part + 1)[...] = (back * swish).astype(jnp.bfloat16)
        column(hidden_ref, part)[...] = hidden.astype(jnp.bfloat16)
        return gate_sum + jnp.sum(hidden * back, axis=1, keepdims=True)

    rows = recv_ref.shape[0]
    gate_sum = lax.fori_loop(0, 2, half, jnp.zeros((rows, 1), jnp.float32))
    gate_ref[...] = jnp.broadcast_to(gate_sum, gate_ref.shape).astype(jnp.bfloat16)
    weight_terms(recv_ref, grads_ref, hidden_ref, 1 - core_ref[0], term_ref)


def weight_terms(recv_ref, grads_ref, hidden_ref, side, out_ref):
    half, columns = out_ref.shape
    unit = columns // 6
    piece = 128
    blocks = min(4, half // piece)

    for at in range(0, half // piece, blocks):
        rows = slice(at * piece, (at + blocks) * piece)

        def pick(offset):
            starts = [
                pl.multiple_of(offset + (2 * (at + j) + side) * piece, piece) for j in range(blocks)
            ]
            return jnp.concatenate([recv_ref[:, pl.ds(start, piece)] for start in starts], axis=1)

        up = lax.dot_general(
            pick(0), grads_ref[...], CONTRACT_ROWS, preferred_element_type=jnp.float32
        )
        down = lax.dot_general(
            pick(2 * half), hidden_ref[...], CONTRACT_ROWS, preferred_element_type=jnp.float32
        )
        for part in range(2):
            base = part * 3 * unit
            out_ref[rows, base : base + 2 * unit] = up[
                :, 2 * part * unit : (2 * part + 2) * unit
            ].astype(out_ref.dtype)
            out_ref[rows, base + 2 * unit : base + 3 * unit] = down[
                :, part * unit : (part + 1) * unit
            ].astype(out_ref.dtype)


def forward(core, recv, own, other):
    rows = recv.shape[0]
    count, piece, columns = own.shape
    width = 2 * count * piece
    return pl.pallas_call(
        forward_kernel,
        out_shape=(
            jax.ShapeDtypeStruct((rows, columns // 6 * 4), jnp.bfloat16),
            jax.ShapeDtypeStruct((rows, columns // 3), jnp.bfloat16),
            jax.ShapeDtypeStruct((rows, 128), jnp.bfloat16),
            jax.ShapeDtypeStruct((width // 2, columns), jnp.bfloat16),
            pltpu.VMEM((count, 2, piece, columns), own.dtype),
        ),
        in_specs=[whole(pltpu.SMEM), whole(), whole(pl.ANY), whole(pl.ANY)],
        out_specs=(whole(),) * 5,
        scratch_shapes=[pltpu.SemaphoreType.DMA((4,))],
        compiler_params=pltpu.CompilerParams(vmem_limit_bytes=FORWARD_LIMIT),
        cost_estimate=cost(3 * rows * width * columns, 14 << 20),
        name="forward",
    )(core, recv, own, other)


def input_kernel(grads_ref, held_ref, gate_ref, out_ref):
    count, _, piece, columns = held_ref.shape
    unit = columns // 6
    width = 2 * count * piece
    chunk = width // 2
    for at in range(2):
        blocks = slice(at * count // 2, (at + 1) * count // 2)
        got = 0.0
        for part in range(2):
            got = got + lax.dot_general(
                grads_ref[:, 2 * part * unit : (2 * part + 2) * unit],
                held_ref[blocks, :, :, 3 * part * unit : (3 * part + 2) * unit].reshape(
                    chunk, 2 * unit
                ),
                CONTRACT_COLS,
                preferred_element_type=jnp.float32,
            )
        out_ref[:, at * chunk : (at + 1) * chunk] = got.astype(jnp.bfloat16)
    out_ref[:, width:] = gate_ref[...]


def input_terms(grads, weights, gate):
    rows = grads.shape[0]
    count, _, piece, columns = weights.shape
    width = 2 * count * piece
    return pl.pallas_call(
        input_kernel,
        out_shape=jax.ShapeDtypeStruct((rows, width + gate.shape[1]), jnp.bfloat16),
        in_specs=[whole()] * 3,
        out_specs=whole(),
        compiler_params=pltpu.CompilerParams(vmem_limit_bytes=20 * MIB),
        cost_estimate=cost(4 * rows * width * columns // 3, 9 << 20),
        name="input_terms",
    )(grads, weights, gate)


def own_kernel(core_ref, recv_ref, grads_ref, hidden_ref, out_ref):
    weight_terms(recv_ref, grads_ref, hidden_ref, core_ref[0], out_ref)


def own_terms(core, recv, grads, hidden, columns):
    rows, width = recv.shape
    return pl.pallas_call(
        own_kernel,
        out_shape=jax.ShapeDtypeStruct((width // 4, columns), jnp.float32),
        in_specs=[whole(pltpu.SMEM)] + [whole()] * 3,
        out_specs=whole(),
        compiler_params=pltpu.CompilerParams(vmem_limit_bytes=20 * MIB),
        cost_estimate=cost(rows * width * columns // 2, 10 * MIB),
        name="own_terms",
    )(core, recv, grads, hidden)


def add_kernel(own_ref, arrived_ref, out_hbm, out_ref, sems):
    count = sems.shape[0]
    rows = out_ref.shape[0] // count
    copies = []
    for i in range(count):
        at = slice(i * rows, (i + 1) * rows)
        total = own_ref[at, :] + arrived_ref[at, :].astype(jnp.float32)
        out_ref[at, :] = total.astype(jnp.bfloat16)
        copies.append(pltpu.make_async_copy(out_ref.at[at], out_hbm.at[at], sems.at[i]))
        copies[-1].start()
    for copy in copies:
        copy.wait()


def add(own, arrived):
    return pl.pallas_call(
        add_kernel,
        out_shape=pltpu.HBM(arrived.shape, jnp.bfloat16),
        in_specs=[whole()] * 2,
        out_specs=whole(pl.ANY),
        scratch_shapes=[pltpu.VMEM(arrived.shape, jnp.bfloat16), pltpu.SemaphoreType.DMA((4,))],
        compiler_params=pltpu.CompilerParams(vmem_limit_bytes=20 * MIB),
        cost_estimate=cost(arrived.size, 12 * MIB),
        name="add",
    )(own, arrived)


def unpack_kernel(back_ref, sum_ref, gate_ref, route_ref, out_ref, gate_out_ref, table_ref, *, capacity):
    layers, tokens = route_ref.shape
    experts = back_ref.shape[0] // (layers * capacity)

    @pl.when(pl.program_id(0) == 0)
    def _():
        match = slot_match(route_ref[...], experts, capacity)
        table_ref[...] = match.astype(jnp.bfloat16)
        sums = sum_ref[:, 0:1].astype(jnp.float32)
        picked = jnp.sum(jnp.where(match, sums, 0.0), axis=0, keepdims=True)
        for layer in range(layers):
            gate = gate_ref[layer : layer + 1, :].astype(jnp.float32)
            value = picked[:, layer * tokens : (layer + 1) * tokens] / gate
            gate_out_ref[layer : layer + 1, :] = value.astype(jnp.bfloat16)

    got = lax.dot_general(
        table_ref[...], back_ref[...], CONTRACT_ROWS, preferred_element_type=jnp.float32
    ).astype(jnp.bfloat16)
    out_ref[...] = got.reshape(out_ref.shape)


def unpack(back, gates, route, capacity):
    rows, columns = back.shape
    layers, tokens = route.shape
    width = columns - 128
    steps = 4
    block = width // steps
    return pl.pallas_call(
        functools.partial(unpack_kernel, capacity=capacity),
        grid=(steps,),
        out_shape=(
            jax.ShapeDtypeStruct((layers, tokens, width), jnp.bfloat16),
            jax.ShapeDtypeStruct((layers, tokens), jnp.bfloat16),
        ),
        in_specs=[
            pl.BlockSpec((rows, block), lambda t: (0, t)),
            pl.BlockSpec((rows, 128), lambda t: (0, width // 128)),
            fixed(gates.shape),
            fixed(route.shape),
        ],
        out_specs=(
            pl.BlockSpec((layers, tokens, block), lambda t: (0, 0, t)),
            fixed((layers, tokens)),
        ),
        scratch_shapes=[pltpu.VMEM((rows, layers * tokens), jnp.bfloat16)],
        compiler_params=pltpu.CompilerParams(vmem_limit_bytes=12 * MIB),
        cost_estimate=cost(2 * rows * layers * tokens * width, 3 << 20),
        name="unpack",
    )(back, back, gates, route)


def finish_kernel(reduced_ref, partner_ref, gate_ref, up_ref, down_ref):
    unit = gate_ref.shape[1]
    for i, ref in enumerate((gate_ref, up_ref, down_ref)):
        at = slice(i * unit, (i + 1) * unit)
        value = reduced_ref[:, at].astype(jnp.float32) + partner_ref[:, at].astype(jnp.float32)
        ref[...] = value if i < 2 else value.T


def finish(reduced, partner):
    piece, columns = partner.shape
    unit = columns // 3
    return pl.pallas_call(
        finish_kernel,
        out_shape=(
            jax.ShapeDtypeStruct((piece, unit), jnp.float32),
            jax.ShapeDtypeStruct((piece, unit), jnp.float32),
            jax.ShapeDtypeStruct((unit, piece), jnp.float32),
        ),
        in_specs=[whole()] * 2,
        out_specs=(whole(),) * 3,
        compiler_params=pltpu.CompilerParams(vmem_limit_bytes=50 * MIB),
        cost_estimate=cost(piece * columns, MIB),
        name="finish",
    )(reduced, partner)


def local(inputs, cotangents, gates, routing, w_gate, w_up, w_down):
    experts = lax.axis_size("e")
    layers, tokens, width = inputs.shape
    capacity = 3 * tokens // (2 * experts)
    unit = w_gate.shape[1]
    route = routing[:, :, 0]
    core = lax.axis_index("c").astype(jnp.int32).reshape(1)
    swap = [(0, 1), (1, 0)]

    sent = pack(inputs, cotangents, gates, route, experts, capacity)
    sent, w_gate = lax.optimization_barrier((sent, w_gate))
    mine = join(w_gate, w_up, w_down)
    paired = lax.ppermute(mine, "k", swap)
    recv = lax.all_to_all(
        sent.reshape(experts, layers * capacity, 2 * width), "e", 0, 0, tiled=True
    ).reshape(experts * layers * capacity, 2 * width)
    own = ring_gather(jnp.concatenate([mine, paired], axis=1))
    other = lax.ppermute(own, "c", swap)

    grads, hidden, gate_sum, term, held = forward(core, recv, own, other)
    arrived = lax.ppermute(term, "c", swap)
    back = input_terms(grads, held, gate_sum)
    hidden, back = lax.optimization_barrier((hidden, back))
    total = own_terms(core, recv, grads, hidden, own.shape[2])
    total = add(total, arrived)
    reduced = lax.psum_scatter(total, "y", scatter_dimension=0, tiled=True)
    back = lax.all_to_all(
        back.reshape(experts, layers * capacity, back.shape[1]), "e", 0, 0, tiled=True
    ).reshape(back.shape)
    grad_inputs, grad_gates = unpack(back, gates, route, capacity)
    partner = lax.ppermute(reduced[:, 3 * unit :], "k", swap)
    return (grad_inputs, grad_gates, *finish(reduced, partner))


def solution(mesh):
    count, peers = mesh.devices.shape
    fine = Mesh(mesh.devices.reshape(count // 2, 2, peers // 2, 2), ("y", "c", "e", "k"))
    dp, expert, both = ("y", "c"), ("e", "k"), ("y", "c", "e", "k")
    return jax.shard_map(
        local,
        mesh=fine,
        in_specs=(
            P(None, both, None),
            P(None, both, None),
            P(None, both),
            P(None, both, None),
            P(dp, expert),
            P(dp, expert),
            P(expert, dp),
        ),
        out_specs=(
            P(None, both, None),
            P(None, both),
            P(dp, expert),
            P(dp, expert),
            P(expert, dp),
        ),
        check_vma=False,
    )
```
